512 devices in a mesh: head: 8 (over y_hi, core), ctx: 64 (over y_lo, z, x).
Axes of the slice: x: 4, y: 8 (y_hi: 4, y_lo: 2; y = y_hi * 2 + y_lo), z: 8, core: 2. Of those that a mesh axis runs over, the one named last changes fastest.
Arguments:
- queries: bfloat16 [32768, 4096], P(('head', 'ctx')), may hold values from -6 to 6
- keys: bfloat16 [32768, 4096], P(('head', 'ctx')), may hold values from -6 to 6
- values: bfloat16 [32768, 4096], P(('head', 'ctx')), may hold values from -6 to 6
- outputs: bfloat16 [32768, 4096], P(('head', 'ctx')), may hold values from -6 to 6
- grad_out: bfloat16 [32768, 4096], P(('head', 'ctx')), may hold values from -235 to 235
- log_totals: float32 [32768, 32], P(('head', 'ctx')), may hold values from 0 to 20
- pair_live: int32 [2, 64], replicated, may hold values from 0 to 1, as said below
Outputs:
- grad_queries: bfloat16 [32768, 4096], P(('head', 'ctx'))
- grad_keys: bfloat16 [32768, 4096], P(('head', 'ctx'))
- grad_values: bfloat16 [32768, 4096], P(('head', 'ctx'))
The draws below stay inside these ranges and needn't reach their ends.
Inputs may be any that keep to these rules, and one draw needn't show every extreme that they name: pair_live[r, c] equals pair_live[r, c XOR (64 / 2^(r + 1))]; in every round some pairs are live and some are not.
All inputs are finite; a program needn't handle non-finite values.
Results may differ from the reference program's by a relative error of at most 0.0065.
Values may be sent and summed in bfloat16 or wider, within the bound.
A program may use at most 64 MiB of HBM per device.

```python
import jax
import jax.numpy as jnp
from jax import lax

H = 32
HD = 128
B = 512
ROUNDS = 2
TOKENS = 32768
N_HEAD = 8
N_CTX = 64


def draw_log_totals(key, part):
    key = jax.random.fold_in(key, 3)
    center = jnp.log(jnp.float32((1 + ROUNDS) * B))
    offset = jax.random.uniform(key, (TOKENS, H), jnp.float32, 0.2, 0.8)
    return center + offset


def draw_pair_live(key, part):
    key = jax.random.fold_in(key, 7)
    count = TOKENS // B
    places = jnp.arange(count, dtype=jnp.int32)
    rounds_list = []
    for step in range(ROUNDS):
        stride = count // 2 ** (step + 1)
        base = jax.random.randint(jax.random.fold_in(key, step), (count,), 0, 4)
        base = base.at[0].set(3).at[count - 1 - stride].set(3).at[1].set(0)
        lower = places - places // stride % 2 * stride
        rounds_list.append((base[lower] > 0).astype(jnp.int32))
    return jnp.stack(rounds_list)


def levels(own_key, shape, pieces, smallest, top_value):
    factor_of = 1.0
    for position, shards_of in pieces:
        heights = jax.random.uniform(jax.random.fold_in(jax.random.fold_in(own_key, 6), position), (shards_of,), jnp.float32, smallest / len(pieces), top_value / len(pieces))
        factor_of = factor_of * jnp.repeat(jnp.exp(heights), shape[position] // shards_of).reshape((-1,) + (1,) * (len(shape) - 1 - position))
    return factor_of


def gaussian(stream_key, extent, scale, bound, cuts=(), kind=jnp.bfloat16):
    values = jax.random.normal(stream_key, extent, jnp.float32) * scale
    if len(cuts) > 0:
        values = levels(stream_key, extent, cuts, -0.22, 0.18) * values
    return jnp.clip(values, min=-bound, max=bound).astype(kind)


def setup_inputs(seed: int = 0) -> dict:
    seeds = jax.random.split(jax.random.key(seed), 8)
    queries = gaussian(seeds[0], (TOKENS, H * HD), 1.0, 6.0, ((0, 512),))
    keys = gaussian(seeds[1], (TOKENS, H * HD), 1.0, 6.0, ((0, 512),))
    values = gaussian(seeds[2], (TOKENS, H * HD), 1.0, 6.0, ((0, 512),))
    outputs = gaussian(seeds[3], (TOKENS, H * HD), 1.0, 6.0, ((0, 512),))
    grad_out = gaussian(seeds[4], (TOKENS, H * HD), ((3 * B) ** 0.5), 235.0, ((0, 512),))
    log_totals = draw_log_totals(jax.random.fold_in(seeds[7], 71), 0)
    pair_live = draw_pair_live(jax.random.fold_in(seeds[7], 71), 0)
    return dict(queries=queries, keys=keys, values=values, outputs=outputs, grad_out=grad_out, log_totals=log_totals, pair_live=pair_live)


def pair_terms(qb, dob, lseb, deltab, kb, vb):
    scale = 1.0 / (qb.shape[-1] ** 0.5)
    scores = jnp.einsum("qhd,khd->hqk", qb.astype(jnp.float32), kb.astype(jnp.float32)) * scale
    probs = jnp.exp(scores - jnp.transpose(lseb)[:, :, None])
    probs_b = probs.astype(jnp.bfloat16)
    grad_v = jnp.einsum("hqk,qhd->khd", probs_b.astype(jnp.float32), dob.astype(jnp.float32))
    grad_p = jnp.einsum("qhd,khd->hqk", dob.astype(jnp.float32), vb.astype(jnp.float32))
    grad_s = (probs * (grad_p - jnp.transpose(deltab)[:, :, None])).astype(jnp.bfloat16)
    grad_q = jnp.einsum("hqk,khd->qhd", grad_s.astype(jnp.float32), kb.astype(jnp.float32)) * scale
    grad_k = jnp.einsum("hqk,qhd->khd", grad_s.astype(jnp.float32), qb.astype(jnp.float32)) * scale
    return grad_q, grad_k, grad_v


def reference(queries, keys, values, outputs, grad_out, log_totals, pair_live):
    run_rows = B // N_HEAD

    def blocks(x, width):
        return x.reshape(N_HEAD, N_CTX, run_rows, width).transpose(1, 0, 2, 3).reshape(N_CTX, B, width)

    def unblock(x):
        width = x.shape[-1]
        return x.reshape(N_CTX, N_HEAD, run_rows, width).transpose(1, 0, 2, 3).reshape(TOKENS, width)

    q_all = blocks(queries, H * HD).reshape(N_CTX, B, H, HD)
    k_all = blocks(keys, H * HD).reshape(N_CTX, B, H, HD)
    v_all = blocks(values, H * HD).reshape(N_CTX, B, H, HD)
    do_all = blocks(grad_out, H * HD).reshape(N_CTX, B, H, HD)
    o_all = blocks(outputs, H * HD).reshape(N_CTX, B, H, HD)
    lse_all = blocks(log_totals, H)
    delta_all = jnp.sum(do_all.astype(jnp.float32) * o_all.astype(jnp.float32), axis=-1)

    def one_block(block):
        grad_q, grad_k, grad_v = pair_terms(q_all[block], do_all[block], lse_all[block], delta_all[block], k_all[block], v_all[block])
        for step in range(ROUNDS):
            partner = jnp.bitwise_xor(block, N_CTX // 2 ** (step + 1))
            live = pair_live[step, block].astype(jnp.float32)
            mine = pair_terms(q_all[block], do_all[block], lse_all[block], delta_all[block], k_all[partner], v_all[partner])
            grad_q = grad_q + live * mine[0]
            theirs = pair_terms(q_all[partner], do_all[partner], lse_all[partner], delta_all[partner], k_all[block], v_all[block])
            grad_k = grad_k + live * theirs[1]
            grad_v = grad_v + live * theirs[2]
        return (grad_q.astype(jnp.bfloat16).reshape(B, H * HD), grad_k.astype(jnp.bfloat16).reshape(B, H * HD), grad_v.astype(jnp.bfloat16).reshape(B, H * HD))

    grad_q, grad_k, grad_v = lax.map(one_block, jnp.arange(N_CTX, dtype=jnp.int32))
    return unblock(grad_q), unblock(grad_k), unblock(grad_v)
```

```python
import functools

import jax
import jax.numpy as jnp
from jax import lax
from jax.experimental import pallas as pl
from jax.experimental.pallas import tpu as pltpu
from jax.sharding import PartitionSpec as P

H = 32
HD = 128
RUN = 64
RUNS = 8
BLOCKS = 4
B = RUN * RUNS
LOG2E = 1.4426950408889634
SCALE = 1.0 / HD**0.5
Q, K, DO, V = 0, 1, 2, 3
NT = (((1,), (1,)), ((), ()))
NN = (((1,), (0,)), ((), ()))
TN = (((0,), (0,)), ((), ()))


def dot(a, b, dims):
    return lax.dot_general(a, b, dims, preferred_element_type=jnp.float32)


def partner(block, step):
    if step == 0:
        return block
    if step == 1:
        return (block + 2) % 4
    return block + 1 - 2 * (block % 2)


def kernel(
    ctx_size,
    live_ref,
    lse_ref,
    q_ref,
    k_ref,
    v_ref,
    o_ref,
    do_ref,
    gq_ref,
    gk_ref,
    gv_ref,
    buf,
    stat,
    stat_src,
    probs,
    grad_s,
    stage,
    rows,
    load_sem,
    send_sem,
    recv_sem,
    stat_sem,
    back_send,
    back_recv,
):
    run = lax.axis_index("head")
    ctx = lax.axis_index("ctx")
    quarter = ctx_size // 4
    rest = ctx % quarter
    block = ctx // quarter
    y_lo = block // 2
    z_hi = block % 2
    y = run // 2 * 2 + y_lo
    core = run % 2
    head = run * 4 + block
    my_columns = pl.ds(pl.multiple_of(head * HD, HD), HD)

    def peer(t):
        p = t // 4
        dy = 4 + (p % 2) * ((p + 1) // 2) - (1 - p % 2) * (p // 2)
        y_there = (y + dy) % 8
        z_there = (z_hi + 1 - t // 2 % 2) % 2
        core_there = (core + 1 - t % 2) % 2
        return y_there // 2 * 2 + core_there, y_there % 2 * 2 + z_there

    def device(run_there, block_there):
        return (run_there, block_there * quarter + rest)

    load_do = pltpu.make_async_copy(do_ref, rows.at[0], load_sem.at[0])
    load_o = pltpu.make_async_copy(o_ref, rows.at[1], load_sem.at[1])
    load_do.start()
    load_o.start()

    barrier = pltpu.get_barrier_semaphore()

    def greet(t, carry):
        run_there, block_there = peer(t)
        pl.semaphore_signal(
            barrier, inc=1, device_id=device(run_there, block_there), device_id_type=pl.DeviceIdType.MESH
        )
        return carry

    lax.fori_loop(0, 31, greet, 0)
    pl.semaphore_wait(barrier, 31)

    def slot(array):
        return buf.at[array, pl.ds(pl.multiple_of((block * RUNS + run) * RUN, RUN), RUN)]

    def send_array(source, array):
        def body(t, carry):
            run_there, block_there = peer(t)
            column = pl.multiple_of((run_there * 4 + block_there) * HD, HD)
            pltpu.make_async_remote_copy(
                src_ref=source.at[:, pl.ds(column, HD)],
                dst_ref=slot(array),
                send_sem=send_sem.at[array],
                recv_sem=recv_sem.at[array],
                device_id=device(run_there, block_there),
                device_id_type=pl.DeviceIdType.MESH,
            ).start()
            return carry

        pltpu.make_async_copy(source.at[:, my_columns], slot(array), recv_sem.at[array]).start()
        lax.fori_loop(0, 31, body, 0)

    send_array(q_ref, Q)
    send_array(k_ref, K)

    load_do.wait()
    load_o.wait()
    lanes = lax.broadcasted_iota(jnp.int32, (8, HD), 1)
    half = jnp.where(lanes // RUN == run % 2, 1.0, 0.0).astype(jnp.float32)
    eye = jnp.where(
        lax.broadcasted_iota(jnp.int32, (H, H), 0) == lax.broadcasted_iota(jnp.int32, (H, H), 1), 1.0, 0.0
    ).astype(jnp.float32)
    lse = lse_ref[...]
    lse_lines = lax.dot_general(
        eye,
        jnp.concatenate([lse, lse], axis=0),
        NT,
        precision=lax.Precision.HIGHEST,
        preferred_element_type=jnp.float32,
    )
    stat_src[:, 0, :] = lse_lines * half[:1]
    ones = jnp.ones((8, 2 * HD), jnp.bfloat16)

    def delta_line(h, carry):
        columns = pl.ds(pl.multiple_of(h * HD, HD), HD)
        product = rows[0, :, columns].astype(jnp.float32) * rows[1, :, columns].astype(jnp.float32)
        high = product.astype(jnp.bfloat16)
        low = (product - high.astype(jnp.float32)).astype(jnp.bfloat16)
        both = jnp.concatenate([high, low], axis=1)
        line = dot(ones, jnp.concatenate([both, both], axis=0), NT) * half
        stat_src[h, 1:2, :] = line[:1]
        return carry

    lax.fori_loop(0, H, delta_line, 0)

    def send_stat(t, carry):
        run_there, block_there = peer(t)
        pltpu.make_async_remote_copy(
            src_ref=stat_src.at[run_there * 4 + block_there],
            dst_ref=stat.at[block * RUNS + run],
            send_sem=stat_sem.at[0],
            recv_sem=stat_sem.at[1],
            device_id=device(run_there, block_there),
            device_id_type=pl.DeviceIdType.MESH,
        ).start()
        return carry

    pltpu.make_async_copy(stat_src.at[head], stat.at[block * RUNS + run], stat_sem.at[1]).start()
    lax.fori_loop(0, 31, send_stat, 0)

    send_array(do_ref, DO)
    send_array(v_ref, V)

    def arrived(array):
        pltpu.make_async_copy(buf.at[array], buf.at[array], recv_sem.at[array]).wait()

    def rows_of(array, index):
        return buf[array, pl.ds(pl.multiple_of(index * B, B), B), :]

    def stat_line(index, which):
        parts = []
        for pair in range(RUNS // 2):
            parts.append(
                stat[index * RUNS + 2 * pair, which : which + 1, :]
                + stat[index * RUNS + 2 * pair + 1, which : which + 1, :]
            )
        return jnp.concatenate(parts, axis=1)

    arrived(Q)
    arrived(K)
    pltpu.make_async_copy(stat, stat, stat_sem.at[1]).wait()

    def probs_of(i, carry):
        line = stat_line(i, 0) * LOG2E
        queries = rows_of(Q, i)
        ctx_i = i * quarter + rest
        for step in range(3):
            offset = line
            if step > 0:
                dead = (1 - live_ref[step - 1, ctx_i]).astype(jnp.float32)
                offset = line + dead * 1e30
            keys = rows_of(K, partner(i, step))
            scores = dot(keys, queries, NT) * (SCALE * LOG2E)
            probs[i * 3 + step] = jnp.exp2(scores - offset)
        return carry

    lax.fori_loop(0, BLOCKS, probs_of, 0)

    def stage_rows(array, index):
        return stage.at[array, pl.ds(pl.multiple_of(index * B, B), B)]

    def send_back(target, array):
        def source(run_there, block_there):
            return stage.at[array, pl.ds(pl.multiple_of((block_there * RUNS + run_there) * RUN, RUN), RUN)]

        def body(t, carry):
            run_there, block_there = peer(t)
            pltpu.make_async_remote_copy(
                src_ref=source(run_there, block_there),
                dst_ref=target.at[:, my_columns],
                send_sem=back_send.at[array],
                recv_sem=back_recv.at[array],
                device_id=device(run_there, block_there),
                device_id_type=pl.DeviceIdType.MESH,
            ).start()
            return carry

        pltpu.make_async_copy(source(run, block), target.at[:, my_columns], back_recv.at[array]).start()
        lax.fori_loop(0, 31, body, 0)

    arrived(DO)

    def grad_v_of(j, carry):
        total = jnp.zeros((B, HD), jnp.float32)
        for step in range(3):
            i = partner(j, step)
            total += dot(probs[i * 3 + step].astype(jnp.bfloat16), rows_of(DO, i), NN)
        stage_rows(2, j)[...] = total.astype(jnp.bfloat16)
        return carry

    lax.fori_loop(0, BLOCKS, grad_v_of, 0)
    send_back(gv_ref, 2)

    arrived(V)

    def grad_k_of(j, carry):
        total = jnp.zeros((B, HD), jnp.float32)
        values = rows_of(V, j)
        for step in range(3):
            i = partner(j, step)
            grad_p = dot(values, rows_of(DO, i), NT)
            grad = (probs[i * 3 + step] * (grad_p - stat_line(i, 1))).astype(jnp.bfloat16)
            grad_s[i * 3 + step] = grad
            total += dot(grad, rows_of(Q, i), NN)
        stage_rows(1, j)[...] = (total * SCALE).astype(jnp.bfloat16)
        return carry

    lax.fori_loop(0, BLOCKS, grad_k_of, 0)
    send_back(gk_ref, 1)

    def grad_q_of(i, carry):
        total = jnp.zeros((B, HD), jnp.float32)
        for step in range(3):
            total += dot(grad_s[i * 3 + step], rows_of(K, partner(i, step)), TN)
        stage_rows(0, i)[...] = (total * SCALE).astype(jnp.bfloat16)
        return carry

    lax.fori_loop(0, BLOCKS, grad_q_of, 0)
    send_back(gq_ref, 0)

    sent = pl.ds(0, 31 * RUN)
    for array in range(4):
        pltpu.make_async_copy(buf.at[array, sent], buf.at[array, sent], send_sem.at[array]).wait()
    pltpu.make_async_copy(stat.at[pl.ds(0, 31)], stat.at[pl.ds(0, 31)], stat_sem.at[0]).wait()
    for array in range(3):
        pltpu.make_async_copy(stage.at[array, sent], stage.at[array, sent], back_send.at[array]).wait()
    for array, target in enumerate((gq_ref, gk_ref, gv_ref)):
        pltpu.make_async_copy(target, target, back_recv.at[array]).wait()


def on_device(queries, keys, values, outputs, grad_out, log_totals, pair_live):
    anywhere = pl.BlockSpec(memory_space=pl.ANY)
    rows = B * BLOCKS
    out = jax.ShapeDtypeStruct(queries.shape, jnp.bfloat16)
    pairs = 3 * BLOCKS
    flops = 10 * pairs * B * B * HD
    return pl.pallas_call(
        functools.partial(kernel, lax.axis_size("ctx")),
        out_shape=(out, out, out),
        in_specs=[
            pl.BlockSpec(memory_space=pltpu.SMEM),
            pl.BlockSpec(memory_space=pltpu.VMEM),
            anywhere,
            anywhere,
            anywhere,
            anywhere,
            anywhere,
        ],
        out_specs=(anywhere, anywhere, anywhere),
        scratch_shapes=[
            pltpu.VMEM((4, rows, HD), jnp.bfloat16),
            pltpu.VMEM((BLOCKS * RUNS, 2, HD), jnp.float32),
            pltpu.VMEM((H, 2, HD), jnp.float32),
            pltpu.VMEM((pairs, B, B), jnp.float32),
            pltpu.VMEM((pairs, B, B), jnp.bfloat16),
            pltpu.VMEM((3, rows, HD), jnp.bfloat16),
            pltpu.VMEM((2, RUN, H * HD), jnp.bfloat16),
            pltpu.SemaphoreType.DMA((2,)),
            pltpu.SemaphoreType.DMA((4,)),
            pltpu.SemaphoreType.DMA((4,)),
            pltpu.SemaphoreType.DMA((2,)),
            pltpu.SemaphoreType.DMA((3,)),
            pltpu.SemaphoreType.DMA((3,)),
        ],
        compiler_params=pltpu.CompilerParams(
            collective_id=0, has_side_effects=True, vmem_limit_bytes=48 * 1024 * 1024
        ),
        cost_estimate=pl.CostEstimate(
            flops=flops, bytes_accessed=8 * RUN * H * HD * 2, transcendentals=pairs * B * B
        ),
        name="pair_attention_backward",
    )(pair_live, log_totals, queries, keys, values, outputs, grad_out)


def solution(mesh):
    rows = P(("head", "ctx"), None)
    return jax.shard_map(
        on_device,
        mesh=mesh,
        in_specs=(rows, rows, rows, rows, rows, rows, P()),
        out_specs=(rows, rows, rows),
        check_vma=False,
    )
```

```python
import functools

import jax
import jax.numpy as jnp
from jax import lax
from jax.experimental import pallas as pl
from jax.experimental.pallas import tpu as pltpu
from jax.sharding import PartitionSpec as P

H = 32
HD = 128
RUN = 64
RUNS = 8
BLOCKS = 4
B = RUN * RUNS
LOG2E = 1.4426950408889634
SCALE = 1.0 / HD**0.5
Q, K, DO, V = 0, 1, 2, 3
NT = (((1,), (1,)), ((), ()))
NN = (((1,), (0,)), ((), ()))
TN = (((0,), (0,)), ((), ()))


def dot(a, b, dims):
    return lax.dot_general(a, b, dims, preferred_element_type=jnp.float32)


def partner(block, step):
    if step == 0:
        return block
    if step == 1:
        return (block + 2) % 4
    return block + 1 - 2 * (block % 2)


def kernel(
    ctx_size,
    live_ref,
    lse_ref,
    q_ref,
    k_ref,
    v_ref,
    o_ref,
    do_ref,
    out_ref,
    buf,
    stat,
    stat_src,
    probs,
    grad_s,
    stage,
    rows,
    lse_rows,
    load_sem,
    send_sem,
    recv_sem,
    stat_sem,
    back_send,
    back_recv,
):
    run = lax.axis_index("head")
    ctx = lax.axis_index("ctx")
    quarter = ctx_size // 4
    rest = ctx % quarter
    block = ctx // quarter
    y_lo = block // 2
    z_hi = block % 2
    y = run // 2 * 2 + y_lo
    core = run % 2
    head = run * 4 + block
    my_columns = pl.ds(pl.multiple_of(head * HD, HD), HD)

    def peer(t):
        p = t // 4
        dy = 4 + (p % 2) * ((p + 1) // 2) - (1 - p % 2) * (p // 2)
        y_there = (y + dy) % 8
        z_there = (z_hi + 1 - t // 2 % 2) % 2
        core_there = (core + 1 - t % 2) % 2
        return y_there // 2 * 2 + core_there, y_there % 2 * 2 + z_there

    def device(run_there, block_there):
        return (run_there, block_there * quarter + rest)

    load_do = pltpu.make_async_copy(do_ref, rows.at[0], load_sem.at[0])
    load_o = pltpu.make_async_copy(o_ref, rows.at[1], load_sem.at[1])
    load_lse = pltpu.make_async_copy(lse_ref, lse_rows, load_sem.at[2])
    load_do.start()
    load_o.start()
    load_lse.start()

    barrier = pltpu.get_barrier_semaphore()

    def greet(t, carry):
        run_there, block_there = peer(t)
        pl.semaphore_signal(
            barrier, inc=1, device_id=device(run_there, block_there), device_id_type=pl.DeviceIdType.MESH
        )
        return carry

    lax.fori_loop(0, 31, greet, 0)
    pl.semaphore_wait(barrier, 31)

    def slot(array):
        return buf.at[array, pl.ds(pl.multiple_of((block * RUNS + run) * RUN, RUN), RUN)]

    def send_array(source, array):
        def body(t, carry):
            run_there, block_there = peer(t)
            column = pl.multiple_of((run_there * 4 + block_there) * HD, HD)
            pltpu.make_async_remote_copy(
                src_ref=source.at[:, pl.ds(column, HD)],
                dst_ref=slot(array),
                send_sem=send_sem.at[array],
                recv_sem=recv_sem.at[array],
                device_id=device(run_there, block_there),
                device_id_type=pl.DeviceIdType.MESH,
            ).start()
            return carry

        pltpu.make_async_copy(source.at[:, my_columns], slot(array), recv_sem.at[array]).start()
        lax.fori_loop(0, 31, body, 0)

    send_array(q_ref, Q)
    send_array(k_ref, K)

    load_do.wait()
    load_o.wait()
    load_lse.wait()
    lanes = lax.broadcasted_iota(jnp.int32, (8, HD), 1)
    half = jnp.where(lanes // RUN == run % 2, 1.0, 0.0).astype(jnp.float32)
    twice = jnp.where(
        lax.broadcasted_iota(jnp.int32, (RUN, HD), 0) == lax.broadcasted_iota(jnp.int32, (RUN, HD), 1) % RUN, 1.0, 0.0
    ).astype(jnp.float32)
    lse_lines = lax.dot_general(
        lse_rows[...], twice, NN, precision=lax.Precision.HIGHEST, preferred_element_type=jnp.float32
    )
    stat_src[:, 0, :] = lse_lines * half[:1]
    ones = jnp.ones((8, 2 * HD), jnp.bfloat16)

    def delta_line(h, carry):
        columns = pl.ds(pl.multiple_of(h * HD, HD), HD)
        product = rows[0, :, columns].astype(jnp.float32) * rows[1, :, columns].astype(jnp.float32)
        high = product.astype(jnp.bfloat16)
        low = (product - high.astype(jnp.float32)).astype(jnp.bfloat16)
        both = jnp.concatenate([high, low], axis=1)
        line = dot(ones, jnp.concatenate([both, both], axis=0), NT) * half
        stat_src[h, 1:2, :] = line[:1]
        return carry

    lax.fori_loop(0, H, delta_line, 0)

    def send_stat(t, carry):
        run_there, block_there = peer(t)
        pltpu.make_async_remote_copy(
            src_ref=stat_src.at[run_there * 4 + block_there],
            dst_ref=stat.at[block * RUNS + run],
            send_sem=stat_sem.at[0],
            recv_sem=stat_sem.at[1],
            device_id=device(run_there, block_there),
            device_id_type=pl.DeviceIdType.MESH,
        ).start()
        return carry

    pltpu.make_async_copy(stat_src.at[head], stat.at[block * RUNS + run], stat_sem.at[1]).start()
    lax.fori_loop(0, 31, send_stat, 0)

    send_array(do_ref, DO)
    send_array(v_ref, V)

    def arrived(array):
        pltpu.make_async_copy(buf.at[array], buf.at[array], recv_sem.at[array]).wait()

    def rows_of(array, index):
        return buf[array, pl.ds(pl.multiple_of(index * B, B), B), :]

    def stat_line(index, which):
        parts = []
        for pair in range(RUNS // 2):
            parts.append(
                stat[index * RUNS + 2 * pair, which : which + 1, :]
                + stat[index * RUNS + 2 * pair + 1, which : which + 1, :]
            )
        return jnp.concatenate(parts, axis=1)

    arrived(Q)
    arrived(K)
    pltpu.make_async_copy(stat, stat, stat_sem.at[1]).wait()

    def probs_of(i, carry):
        line = stat_line(i, 0) * LOG2E
        queries = rows_of(Q, i)
        ctx_i = i * quarter + rest
        for step in range(3):
            offset = line
            if step > 0:
                dead = (1 - live_ref[step - 1, ctx_i]).astype(jnp.float32)
                offset = line + dead * 1e30
            keys = rows_of(K, partner(i, step))
            scores = dot(keys, queries, NT) * (SCALE * LOG2E)
            probs[i * 3 + step] = jnp.exp2(scores - offset)
        return carry

    lax.fori_loop(0, BLOCKS, probs_of, 0)

    def stage_rows(array, index):
        return stage.at[array, pl.ds(pl.multiple_of(index * B, B), B)]

    def send_back(array):
        target = out_ref.at[array]

        def source(run_there, block_there):
            return stage.at[array, pl.ds(pl.multiple_of((block_there * RUNS + run_there) * RUN, RUN), RUN)]

        def body(t, carry):
            run_there, block_there = peer(t)
            pltpu.make_async_remote_copy(
                src_ref=source(run_there, block_there),
                dst_ref=target.at[:, my_columns],
                send_sem=back_send.at[array],
                recv_sem=back_recv.at[array],
                device_id=device(run_there, block_there),
                device_id_type=pl.DeviceIdType.MESH,
            ).start()
            return carry

        pltpu.make_async_copy(source(run, block), target.at[:, my_columns], back_recv.at[array]).start()
        lax.fori_loop(0, 31, body, 0)

    arrived(DO)

    def grad_v_of(j, carry):
        total = jnp.zeros((B, HD), jnp.float32)
        for step in range(3):
            i = partner(j, step)
            total += dot(probs[i * 3 + step].astype(jnp.bfloat16), rows_of(DO, i), NN)
        stage_rows(2, j)[...] = total.astype(jnp.bfloat16)
        return carry

    lax.fori_loop(0, BLOCKS, grad_v_of, 0)
    send_back(2)

    arrived(V)

    def grad_k_of(j, carry):
        total = jnp.zeros((B, HD), jnp.float32)
        values = rows_of(V, j)
        for step in range(3):
            i = partner(j, step)
            grad_p = dot(values, rows_of(DO, i), NT)
            grad = (probs[i * 3 + step] * (grad_p - stat_line(i, 1))).astype(jnp.bfloat16)
            grad_s[i * 3 + step] = grad
            total += dot(grad, rows_of(Q, i), NN)
        stage_rows(1, j)[...] = (total * SCALE).astype(jnp.bfloat16)
        return carry

    lax.fori_loop(0, BLOCKS, grad_k_of, 0)
    send_back(1)

    def grad_q_of(i, carry):
        total = jnp.zeros((B, HD), jnp.float32)
        for step in range(3):
            total += dot(grad_s[i * 3 + step], rows_of(K, partner(i, step)), TN)
        stage_rows(0, i)[...] = (total * SCALE).astype(jnp.bfloat16)
        return carry

    lax.fori_loop(0, BLOCKS, grad_q_of, 0)
    send_back(0)

    sent = pl.ds(0, 31 * RUN)
    for array in range(4):
        pltpu.make_async_copy(buf.at[array, sent], buf.at[array, sent], send_sem.at[array]).wait()
    pltpu.make_async_copy(stat.at[pl.ds(0, 31)], stat.at[pl.ds(0, 31)], stat_sem.at[0]).wait()
    for array in range(3):
        pltpu.make_async_copy(stage.at[array, sent], stage.at[array, sent], back_send.at[array]).wait()
    for array in range(3):
        pltpu.make_async_copy(out_ref.at[array], out_ref.at[array], back_recv.at[array]).wait()


def on_device(queries, keys, values, outputs, grad_out, log_totals, pair_live):
    anywhere = pl.BlockSpec(memory_space=pl.ANY)
    rows = B * BLOCKS
    pairs = 3 * BLOCKS
    flops = 10 * pairs * B * B * HD
    grads = pl.pallas_call(
        functools.partial(kernel, lax.axis_size("ctx")),
        out_shape=jax.ShapeDtypeStruct((3, *queries.shape), jnp.bfloat16),
        in_specs=[
            pl.BlockSpec(memory_space=pltpu.SMEM),
            anywhere,
            anywhere,
            anywhere,
            anywhere,
            anywhere,
            anywhere,
        ],
        out_specs=anywhere,
        scratch_shapes=[
            pltpu.VMEM((4, rows, HD), jnp.bfloat16),
            pltpu.VMEM((BLOCKS * RUNS, 2, HD), jnp.float32),
            pltpu.VMEM((H, 2, HD), jnp.float32),
            pltpu.VMEM((pairs, B, B), jnp.float32),
            pltpu.VMEM((pairs, B, B), jnp.bfloat16),
            pltpu.VMEM((3, rows, HD), jnp.bfloat16),
            pltpu.VMEM((2, RUN, H * HD), jnp.bfloat16),
            pltpu.VMEM((H, RUN), jnp.float32),
            pltpu.SemaphoreType.DMA((3,)),
            pltpu.SemaphoreType.DMA((4,)),
            pltpu.SemaphoreType.DMA((4,)),
            pltpu.SemaphoreType.DMA((2,)),
            pltpu.SemaphoreType.DMA((3,)),
            pltpu.SemaphoreType.DMA((3,)),
        ],
        compiler_params=pltpu.CompilerParams(
            collective_id=0, has_side_effects=True, vmem_limit_bytes=63 * 1024 * 1024
        ),
        cost_estimate=pl.CostEstimate(
            flops=flops, bytes_accessed=8 * RUN * H * HD * 2, transcendentals=pairs * B * B
        ),
        name="pair_attention_backward",
    )(pair_live, jnp.transpose(log_totals), queries, keys, values, outputs, grad_out)
    return grads[0], grads[1], grads[2]


def solution(mesh):
    rows = P(("head", "ctx"), None)
    return jax.shard_map(
        on_device,
        mesh=mesh,
        in_specs=(rows, rows, rows, rows, rows, rows, P()),
        out_specs=(rows, rows, rows),
        check_vma=False,
    )
```

```python
import functools

import jax
import jax.numpy as jnp
from jax import lax
from jax.experimental import pallas as pl
from jax.experimental.pallas import tpu as pltpu
from jax.sharding import PartitionSpec as P

H = 32
HD = 128
RUN = 64
RUNS = 8
BLOCKS = 4
B = RUN * RUNS
LOG2E = 1.4426950408889634
SCALE = 1.0 / HD**0.5
Q, K, DO, V = 0, 1, 2, 3
NT = (((1,), (1,)), ((), ()))
NN = (((1,), (0,)), ((), ()))
TN = (((0,), (0,)), ((), ()))


def dot(a, b, dims):
    return lax.dot_general(a, b, dims, preferred_element_type=jnp.float32)


def partner(block, step):
    if step == 0:
        return block
    if step == 1:
        return block + 1 - 2 * (block % 2)
    return (block + 2) % 4


def kernel(
    ctx_size,
    live_ref,
    lse_ref,
    q_ref,
    k_ref,
    v_ref,
    o_ref,
    do_ref,
    out_ref,
    buf,
    relay,
    stat,
    stat_src,
    stat_relay,
    probs,
    grad_s,
    stage,
    relay_back,
    rows,
    lse_rows,
    load_sem,
    send_sem,
    recv_sem,
    across_send,
    across_recv,
    stat_sem,
    back_send,
    back_recv,
    back_across_send,
    back_across_recv,
):
    run = lax.axis_index("head")
    ctx = lax.axis_index("ctx")
    quarter = ctx_size // 4
    rest = ctx % quarter
    y_lo = ctx // quarter // 2
    z_hi = ctx // quarter % 2
    y = run // 2 * 2 + y_lo
    core = run % 2
    z_other = 1 - z_hi
    block = z_hi * 2 + y_lo
    block_across = z_other * 2 + y_lo

    def head(z_there, core_there, y_there):
        return z_there * 16 + core_there * 8 + y_there

    def columns(index, count=1):
        return pl.ds(pl.multiple_of(index * HD, HD), count * HD)

    def device(y_there, core_there, z_there):
        ctx_there = (y_there % 2 * 2 + z_there) * quarter + rest
        return (y_there // 2 * 2 + core_there, ctx_there)

    def send(source, target, sent, received, where):
        pltpu.make_async_remote_copy(
            src_ref=source,
            dst_ref=target,
            send_sem=sent,
            recv_sem=received,
            device_id=where,
            device_id_type=pl.DeviceIdType.MESH,
        ).start()

    def y_at(p):
        return (y + 4 + (p % 2) * ((p + 1) // 2) - (1 - p % 2) * (p // 2)) % 8

    across = device(y, core, z_other)

    def each(first, last, body):
        lax.fori_loop(first, last, lambda t, carry: (body(t), carry)[1], 0)

    load_do = pltpu.make_async_copy(do_ref, rows.at[0], load_sem.at[0])
    load_o = pltpu.make_async_copy(o_ref, rows.at[1], load_sem.at[1])
    load_lse = pltpu.make_async_copy(lse_ref, lse_rows, load_sem.at[2])
    load_do.start()
    load_o.start()
    load_lse.start()

    barrier = pltpu.get_barrier_semaphore()

    def greet(where):
        pl.semaphore_signal(barrier, inc=1, device_id=where, device_id_type=pl.DeviceIdType.MESH)

    greet(across)
    each(0, 15, lambda t: greet(device(y_at(t // 2), (core + 1 - t % 2) % 2, z_hi)))
    pl.semaphore_wait(barrier, 16)

    def slot(array, from_block):
        return buf.at[array, pl.ds(pl.multiple_of((from_block * RUNS + run) * RUN, RUN), RUN)]

    def send_across(source, array):
        for piece in range(2):
            core_there = (core + 1 - piece) % 2
            send(
                source.at[:, columns(head(z_other, core_there, 0), 8)],
                relay.at[array, piece],
                across_send.at[0],
                across_recv.at[array * 2 + piece],
                across,
            )

    def send_column(source, array):
        def body(t):
            y_there, core_there = y_at(t // 2), (core + 1 - t % 2) % 2
            send(
                source.at[:, columns(head(z_hi, core_there, y_there))],
                slot(array, block),
                send_sem.at[array],
                recv_sem.at[array],
                device(y_there, core_there, z_hi),
            )

        mine = source.at[:, columns(head(z_hi, core, y))]
        pltpu.make_async_copy(mine, slot(array, block), recv_sem.at[array]).start()
        each(0, 15, body)

    def forward(array, piece):
        core_there = (core + 1 - piece) % 2
        arrival = relay.at[array, piece]
        pltpu.make_async_copy(arrival, arrival, across_recv.at[array * 2 + piece]).wait()

        def body(p):
            y_there = y_at(p)
            send(
                arrival.at[:, columns(y_there)],
                slot(array, block_across),
                send_sem.at[array],
                recv_sem.at[array],
                device(y_there, core_there, z_hi),
            )

        if piece == 1:
            mine = arrival.at[:, columns(y)]
            pltpu.make_async_copy(mine, slot(array, block_across), recv_sem.at[array]).start()
        each(0, 8 - piece, body)

    send_across(q_ref, Q)
    send_across(k_ref, K)
    send_column(q_ref, Q)
    send_column(k_ref, K)

    load_do.wait()
    load_o.wait()
    load_lse.wait()
    lanes = lax.broadcasted_iota(jnp.int32, (8, HD), 1)
    half = jnp.where(lanes // RUN == run % 2, 1.0, 0.0).astype(jnp.float32)
    twice = jnp.where(
        lax.broadcasted_iota(jnp.int32, (RUN, HD), 0) == lax.broadcasted_iota(jnp.int32, (RUN, HD), 1) % RUN, 1.0, 0.0
    ).astype(jnp.float32)
    lse_lines = lax.dot_general(
        lse_rows[...], twice, NN, precision=lax.Precision.HIGHEST, preferred_element_type=jnp.float32
    )
    stat_src[:, 0, :] = lse_lines * half[:1]
    ones = jnp.ones((8, 2 * HD), jnp.bfloat16)

    def delta_line(h):
        product = rows[0, :, columns(h)].astype(jnp.float32) * rows[1, :, columns(h)].astype(jnp.float32)
        high = product.astype(jnp.bfloat16)
        low = (product - high.astype(jnp.float32)).astype(jnp.bfloat16)
        both = jnp.concatenate([high, low], axis=1)
        line = dot(ones, jnp.concatenate([both, both], axis=0), NT) * half
        stat_src[h, 1:2, :] = line[:1]

    each(0, H, delta_line)

    def stat_slot(from_block):
        return stat.at[from_block * RUNS + run]

    def send_stat(source, from_block):
        def body(t):
            y_there, core_there = y_at(t // 2), (core + 1 - t % 2) % 2
            send(
                source(core_there, y_there),
                stat_slot(from_block),
                stat_sem.at[0],
                stat_sem.at[1],
                device(y_there, core_there, z_hi),
            )

        pltpu.make_async_copy(source(core, y), stat_slot(from_block), stat_sem.at[1]).start()
        each(0, 15, body)

    send(stat_src.at[pl.ds(z_other * 16, 16)], stat_relay, stat_sem.at[2], stat_sem.at[3], across)
    send_across(do_ref, DO)
    send_across(v_ref, V)
    send_stat(lambda core_there, y_there: stat_src.at[head(z_hi, core_there, y_there)], block)
    send_column(do_ref, DO)
    forward(Q, 0)
    forward(Q, 1)
    send_column(v_ref, V)
    forward(K, 0)
    forward(K, 1)
    pltpu.make_async_copy(stat_relay, stat_relay, stat_sem.at[3]).wait()
    send_stat(lambda core_there, y_there: stat_relay.at[head(0, core_there, y_there)], block_across)
    forward(DO, 0)

    def arrived(array):
        pltpu.make_async_copy(buf.at[array], buf.at[array], recv_sem.at[array]).wait()

    def rows_of(array, index):
        return buf[array, pl.ds(pl.multiple_of(index * B, B), B), :]

    def stat_line(index, which):
        parts = []
        for pair in range(RUNS // 2):
            parts.append(
                stat[index * RUNS + 2 * pair, which : which + 1, :]
                + stat[index * RUNS + 2 * pair + 1, which : which + 1, :]
            )
        return jnp.concatenate(parts, axis=1)

    arrived(Q)
    arrived(K)
    pltpu.make_async_copy(stat, stat, stat_sem.at[1]).wait()

    def probs_of(i):
        line = stat_line(i, 0) * LOG2E
        queries = rows_of(Q, i)
        ctx_i = (i % 2 * 2 + i // 2) * quarter + rest
        for step in range(3):
            offset = line
            if step > 0:
                dead = (1 - live_ref[step - 1, ctx_i]).astype(jnp.float32)
                offset = line + dead * 1e30
            keys = rows_of(K, partner(i, step))
            scores = dot(keys, queries, NT) * (SCALE * LOG2E)
            probs[i * 3 + step] = jnp.exp2(scores - offset)

    each(0, BLOCKS, probs_of)
    forward(DO, 1)
    forward(V, 0)

    def staged(array, index):
        return stage.at[array, pl.ds(pl.multiple_of(index * B, B), B)]

    def staged_run(array, index, run_there):
        return stage.at[array, pl.ds(pl.multiple_of((index * RUNS + run_there) * RUN, RUN), RUN)]

    def send_back(array):
        for piece in range(2):
            send(
                staged(array, z_other * 2 + (y_lo + piece) % 2),
                relay_back.at[array, piece],
                back_across_send.at[0],
                back_across_recv.at[array * 2 + piece],
                across,
            )
        target = out_ref.at[array, :, columns(head(z_hi, core, y))]

        def body(t):
            y_there, core_there = y_at(t // 2), (core + 1 - t % 2) % 2
            send(
                staged_run(array, z_hi * 2 + y_there % 2, y_there // 2 * 2 + core_there),
                target,
                back_send.at[array],
                back_recv.at[array],
                device(y_there, core_there, z_hi),
            )

        pltpu.make_async_copy(staged_run(array, block, run), target, back_recv.at[array]).start()
        each(0, 15, body)

    def forward_back(array, piece):
        arrival = relay_back.at[array, piece]
        pltpu.make_async_copy(arrival, arrival, back_across_recv.at[array * 2 + piece]).wait()
        target = out_ref.at[array, :, columns(head(z_other, core, y))]

        def part(run_there):
            return arrival.at[pl.ds(pl.multiple_of(run_there * RUN, RUN), RUN)]

        def body(t):
            y_there = (y + 4 + 2 * (t // 2) + piece) % 8
            core_there = (core + 1 - t % 2) % 2
            send(
                part(y_there // 2 * 2 + core_there),
                target,
                back_send.at[array],
                back_recv.at[array],
                device(y_there, core_there, z_hi),
            )

        if piece == 0:
            pltpu.make_async_copy(part(run), target, back_recv.at[array]).start()
            each(0, 5, body)
            each(6, 8, body)
        else:
            each(0, 8, body)

    arrived(DO)

    def grad_v_of(j):
        total = jnp.zeros((B, HD), jnp.float32)
        for step in range(3):
            i = partner(j, step)
            total += dot(probs[i * 3 + step].astype(jnp.bfloat16), rows_of(DO, i), NN)
        staged(2, j)[...] = total.astype(jnp.bfloat16)

    each(0, BLOCKS, grad_v_of)
    send_back(2)
    forward(V, 1)
    arrived(V)

    def grad_k_of(j):
        total = jnp.zeros((B, HD), jnp.float32)
        values = rows_of(V, j)
        for step in range(3):
            i = partner(j, step)
            grad_p = dot(values, rows_of(DO, i), NT)
            grad = (probs[i * 3 + step] * (grad_p - stat_line(i, 1))).astype(jnp.bfloat16)
            grad_s[i * 3 + step] = grad
            total += dot(grad, rows_of(Q, i), NN)
        staged(1, j)[...] = (total * SCALE).astype(jnp.bfloat16)

    each(0, BLOCKS, grad_k_of)
    send_back(1)
    forward_back(2, 0)

    def grad_q_of(i):
        total = jnp.zeros((B, HD), jnp.float32)
        for step in range(3):
            total += dot(grad_s[i * 3 + step], rows_of(K, partner(i, step)), TN)
        staged(0, i)[...] = (total * SCALE).astype(jnp.bfloat16)

    each(0, BLOCKS, grad_q_of)
    send_back(0)
    forward_back(2, 1)
    for array in (1, 0):
        for piece in range(2):
            forward_back(array, piece)

    sent = pl.ds(0, 30 * RUN)
    for array in range(4):
        pltpu.make_async_copy(buf.at[array, sent], buf.at[array, sent], send_sem.at[array]).wait()
    pltpu.make_async_copy(relay, relay, across_send.at[0]).wait()
    pltpu.make_async_copy(stat.at[pl.ds(0, 30)], stat.at[pl.ds(0, 30)], stat_sem.at[0]).wait()
    pltpu.make_async_copy(stat_relay, stat_relay, stat_sem.at[2]).wait()
    pltpu.make_async_copy(relay_back, relay_back, back_across_send.at[0]).wait()
    for array in range(3):
        pltpu.make_async_copy(stage.at[array, sent], stage.at[array, sent], back_send.at[array]).wait()
    for array in range(3):
        pltpu.make_async_copy(out_ref.at[array], out_ref.at[array], back_recv.at[array]).wait()


def on_device(queries, keys, values, outputs, grad_out, log_totals, pair_live):
    anywhere = pl.BlockSpec(memory_space=pl.ANY)
    rows = B * BLOCKS
    pairs = 3 * BLOCKS
    flops = 10 * pairs * B * B * HD
    grads = pl.pallas_call(
        functools.partial(kernel, lax.axis_size("ctx")),
        out_shape=jax.ShapeDtypeStruct((3, *queries.shape), jnp.bfloat16),
        in_specs=[
            pl.BlockSpec(memory_space=pltpu.SMEM),
            anywhere,
            anywhere,
            anywhere,
            anywhere,
            anywhere,
            anywhere,
        ],
        out_specs=anywhere,
        scratch_shapes=[
            pltpu.VMEM((4, rows, HD), jnp.bfloat16),
            pltpu.VMEM((4, 2, RUN, 8 * HD), jnp.bfloat16),
            pltpu.VMEM((BLOCKS * RUNS, 2, HD), jnp.float32),
            pltpu.VMEM((H, 2, HD), jnp.float32),
            pltpu.VMEM((H // 2, 2, HD), jnp.float32),
            pltpu.VMEM((pairs, B, B), jnp.float32),
            pltpu.VMEM((pairs, B, B), jnp.bfloat16),
            pltpu.VMEM((3, rows, HD), jnp.bfloat16),
            pltpu.VMEM((3, 2, B, HD), jnp.bfloat16),
            pltpu.VMEM((2, RUN, H * HD), jnp.bfloat16),
            pltpu.VMEM((H, RUN), jnp.float32),
            pltpu.SemaphoreType.DMA((3,)),
            pltpu.SemaphoreType.DMA((4,)),
            pltpu.SemaphoreType.DMA((4,)),
            pltpu.SemaphoreType.DMA((1,)),
            pltpu.SemaphoreType.DMA((8,)),
            pltpu.SemaphoreType.DMA((4,)),
            pltpu.SemaphoreType.DMA((3,)),
            pltpu.SemaphoreType.DMA((3,)),
            pltpu.SemaphoreType.DMA((1,)),
            pltpu.SemaphoreType.DMA((6,)),
        ],
        compiler_params=pltpu.CompilerParams(
            collective_id=0, has_side_effects=True, vmem_limit_bytes=63 * 1024 * 1024
        ),
        cost_estimate=pl.CostEstimate(
            flops=flops, bytes_accessed=8 * RUN * H * HD * 2, transcendentals=pairs * B * B
        ),
        name="pair_attention_backward",
    )(pair_live, jnp.transpose(log_totals), queries, keys, values, outputs, grad_out)
    return grads[0], grads[1], grads[2]


def solution(mesh):
    rows = P(("head", "ctx"), None)
    return jax.shard_map(
        on_device,
        mesh=mesh,
        in_specs=(rows, rows, rows, rows, rows, rows, P()),
        out_specs=(rows, rows, rows),
        check_vma=False,
    )
```

```python
import functools

import jax
import jax.numpy as jnp
from jax import lax
from jax.experimental import pallas as pl
from jax.experimental.pallas import tpu as pltpu
from jax.sharding import PartitionSpec as P

H = 32
HD = 128
RUN = 64
RUNS = 8
BLOCKS = 4
B = RUN * RUNS
LOG2E = 1.4426950408889634
SCALE = 1.0 / HD**0.5
Q, K, DO, V = 0, 1, 2, 3
COLUMN, PARTNERS, BOTH = 0, 1, 2
NT = (((1,), (1,)), ((), ()))
NN = (((1,), (0,)), ((), ()))
TN = (((0,), (0,)), ((), ()))


def dot(a, b, dims):
    return lax.dot_general(a, b, dims, preferred_element_type=jnp.float32)


def partner(block, step):
    if step == 0:
        return block
    if step == 1:
        return block + 1 - 2 * (block % 2)
    return (block + 2) % 4


def kernel(
    ctx_size,
    live_ref,
    lse_ref,
    q_ref,
    k_ref,
    v_ref,
    o_ref,
    do_ref,
    out_ref,
    buf,
    relay,
    stat,
    stat_src,
    probs,
    grad_s,
    stage,
    rows,
    lse_rows,
    load_sem,
    send_sem,
    recv_sem,
    across_send,
    across_recv,
    stat_sem,
    back_send,
    back_recv,
):
    run = lax.axis_index("head")
    ctx = lax.axis_index("ctx")
    quarter = ctx_size // 4
    rest = ctx % quarter
    y_lo = ctx // quarter // 2
    z_hi = ctx // quarter % 2
    y = run // 2 * 2 + y_lo
    core = run % 2
    z_other = 1 - z_hi
    block = z_hi * 2 + y_lo
    block_across = z_other * 2 + y_lo

    def head(z_there, core_there, y_there):
        return z_there * 16 + core_there * 8 + y_there

    def columns(index, count=1):
        return pl.ds(pl.multiple_of(index * HD, HD), count * HD)

    def device(y_there, core_there, z_there):
        ctx_there = (y_there % 2 * 2 + z_there) * quarter + rest
        return (y_there // 2 * 2 + core_there, ctx_there)

    def send(source, target, sent, received, where):
        pltpu.make_async_remote_copy(
            src_ref=source,
            dst_ref=target,
            send_sem=sent,
            recv_sem=received,
            device_id=where,
            device_id_type=pl.DeviceIdType.MESH,
        ).start()

    def y_at(p):
        return (y + 4 + (p % 2) * ((p + 1) // 2) - (1 - p % 2) * (p // 2)) % 8

    across = device(y, core, z_other)

    def each(first, last, body):
        lax.fori_loop(first, last, lambda t, carry: (body(t), carry)[1], 0)

    barrier = pltpu.get_barrier_semaphore()

    def greet(where):
        pl.semaphore_signal(barrier, inc=1, device_id=where, device_id_type=pl.DeviceIdType.MESH)

    greet(across)
    each(0, 15, lambda t: greet(device(y_at(t // 2), (core + 1 - t % 2) % 2, z_hi)))
    load_do = pltpu.make_async_copy(do_ref, rows.at[0], load_sem.at[0])
    load_o = pltpu.make_async_copy(o_ref, rows.at[1], load_sem.at[1])
    load_lse = pltpu.make_async_copy(lse_ref, lse_rows, load_sem.at[2])
    load_do.start()
    load_o.start()
    load_lse.start()
    pl.semaphore_wait(barrier, 16)

    def slot(array, from_block):
        return buf.at[array, pl.ds(pl.multiple_of((from_block * RUNS + run) * RUN, RUN), RUN)]

    def send_across(source):
        for piece in range(2):
            core_there = (core + 1 - piece) % 2
            send(
                source.at[:, columns(head(z_other, core_there, 0), 8)],
                relay.at[piece],
                across_send.at[0],
                across_recv.at[piece],
                across,
            )

    def send_rows(source, array, reach):
        def body(t):
            if reach == BOTH:
                y_there, core_there = y_at(t // 4), (core + 1 - t % 2) % 2
                z_there = (z_hi + 1 - t // 2 % 2) % 2
            else:
                y_there, core_there = y_at(t // 2), (core + 1 - t % 2) % 2
                z_there = z_hi if reach == COLUMN else z_other
            send(
                source.at[:, columns(head(z_there, core_there, y_there))],
                slot(array, block),
                send_sem.at[array],
                recv_sem.at[array],
                device(y_there, core_there, z_there),
            )

        if reach != PARTNERS:
            mine = source.at[:, columns(head(z_hi, core, y))]
            pltpu.make_async_copy(mine, slot(array, block), recv_sem.at[array]).start()
        each(0, {COLUMN: 15, PARTNERS: 16, BOTH: 31}[reach], body)

    def forward(piece):
        core_there = (core + 1 - piece) % 2
        arrival = relay.at[piece]
        pltpu.make_async_copy(arrival, arrival, across_recv.at[piece]).wait()

        def body(p):
            y_there = y_at(p)
            send(
                arrival.at[:, columns(y_there)],
                slot(Q, block_across),
                send_sem.at[Q],
                recv_sem.at[Q],
                device(y_there, core_there, z_hi),
            )

        if piece == 1:
            pltpu.make_async_copy(arrival.at[:, columns(y)], slot(Q, block_across), recv_sem.at[Q]).start()
        each(0, 8 - piece, body)

    send_across(q_ref)
    send_rows(q_ref, Q, COLUMN)
    send_rows(k_ref, K, COLUMN)

    load_do.wait()
    load_o.wait()
    load_lse.wait()
    lanes = lax.broadcasted_iota(jnp.int32, (8, HD), 1)
    half = jnp.where(lanes // RUN == run % 2, 1.0, 0.0).astype(jnp.float32)
    twice = jnp.where(
        lax.broadcasted_iota(jnp.int32, (RUN, HD), 0) == lax.broadcasted_iota(jnp.int32, (RUN, HD), 1) % RUN, 1.0, 0.0
    ).astype(jnp.float32)
    lse_lines = lax.dot_general(
        lse_rows[...], twice, NN, precision=lax.Precision.HIGHEST, preferred_element_type=jnp.float32
    )
    stat_src[:, 0, :] = lse_lines * half[:1]
    ones = jnp.ones((8, 2 * HD), jnp.bfloat16)

    def delta_line(h):
        product = rows[0, :, columns(h)].astype(jnp.float32) * rows[1, :, columns(h)].astype(jnp.float32)
        high = product.astype(jnp.bfloat16)
        low = (product - high.astype(jnp.float32)).astype(jnp.bfloat16)
        both = jnp.concatenate([high, low], axis=1)
        line = dot(ones, jnp.concatenate([both, both], axis=0), NT) * half
        stat_src[h, 1:2, :] = line[:1]

    each(0, H, delta_line)

    forward(0)

    def send_stat(t):
        y_there, core_there = y_at(t // 4), (core + 1 - t % 2) % 2
        z_there = (z_hi + 1 - t // 2 % 2) % 2
        send(
            stat_src.at[head(z_there, core_there, y_there)],
            stat.at[block * RUNS + run],
            stat_sem.at[0],
            stat_sem.at[1],
            device(y_there, core_there, z_there),
        )

    pltpu.make_async_copy(stat_src.at[head(z_hi, core, y)], stat.at[block * RUNS + run], stat_sem.at[1]).start()
    each(0, 31, send_stat)
    send_rows(k_ref, K, PARTNERS)
    forward(1)
    send_rows(do_ref, DO, BOTH)
    send_rows(v_ref, V, BOTH)

    def arrived(array):
        pltpu.make_async_copy(buf.at[array], buf.at[array], recv_sem.at[array]).wait()

    def rows_of(array, index):
        return buf[array, pl.ds(pl.multiple_of(index * B, B), B), :]

    def stat_line(index, which):
        parts = []
        for pair in range(RUNS // 2):
            parts.append(
                stat[index * RUNS + 2 * pair, which : which + 1, :]
                + stat[index * RUNS + 2 * pair + 1, which : which + 1, :]
            )
        return jnp.concatenate(parts, axis=1)

    arrived(Q)
    arrived(K)
    pltpu.make_async_copy(stat, stat, stat_sem.at[1]).wait()

    def probs_of(i):
        line = stat_line(i, 0) * LOG2E
        queries = rows_of(Q, i)
        ctx_i = (i % 2 * 2 + i // 2) * quarter + rest
        for step in range(3):
            offset = line
            if step > 0:
                dead = (1 - live_ref[step - 1, ctx_i]).astype(jnp.float32)
                offset = line + dead * 1e30
            keys = rows_of(K, partner(i, step))
            scores = dot(keys, queries, NT) * (SCALE * LOG2E)
            probs[i * 3 + step] = jnp.exp2(scores - offset)

    each(0, BLOCKS, probs_of)

    def staged(array, index):
        return stage.at[array, pl.ds(pl.multiple_of(index * B, B), B)]

    def staged_run(array, index, run_there):
        return stage.at[array, pl.ds(pl.multiple_of((index * RUNS + run_there) * RUN, RUN), RUN)]

    def give_back(array, result_of):
        target = out_ref.at[array, :, columns(head(z_hi, core, y))]

        def one_block(t):
            z_there = (z_hi + 1 - t % 2) % 2
            odd = 1 - t // 2
            index = z_there * 2 + (y_lo + odd) % 2
            staged(array, index)[...] = result_of(index).astype(jnp.bfloat16)

            def body(u):
                q = u // 2
                y_there = y_at(4 * (q // 2) + (q % 2) * (3 - 2 * odd) + odd)
                core_there = (core + 1 - u % 2) % 2
                send(
                    staged_run(array, index, y_there // 2 * 2 + core_there),
                    target,
                    back_send.at[array],
                    back_recv.at[array],
                    device(y_there, core_there, z_there),
                )

            each(0, 8 - t // 3, body)

        each(0, BLOCKS, one_block)
        pltpu.make_async_copy(staged_run(array, block, run), target, back_recv.at[array]).start()

    arrived(DO)

    def grad_v_of(j):
        total = jnp.zeros((B, HD), jnp.float32)
        for step in range(3):
            i = partner(j, step)
            total += dot(probs[i * 3 + step].astype(jnp.bfloat16), rows_of(DO, i), NN)
        return total

    give_back(2, grad_v_of)
    arrived(V)

    def grad_k_of(j):
        total = jnp.zeros((B, HD), jnp.float32)
        values = rows_of(V, j)
        for step in range(3):
            i = partner(j, step)
            grad_p = dot(values, rows_of(DO, i), NT)
            grad = (probs[i * 3 + step] * (grad_p - stat_line(i, 1))).astype(jnp.bfloat16)
            grad_s[i * 3 + step] = grad
            total += dot(grad, rows_of(Q, i), NN)
        return total * SCALE

    give_back(1, grad_k_of)

    def grad_q_of(i):
        total = jnp.zeros((B, HD), jnp.float32)
        for step in range(3):
            total += dot(grad_s[i * 3 + step], rows_of(K, partner(i, step)), TN)
        return total * SCALE

    give_back(0, grad_q_of)

    for array in range(4):
        sent = buf.at[array, pl.ds(0, (30 if array == Q else 31) * RUN)]
        pltpu.make_async_copy(sent, sent, send_sem.at[array]).wait()
    pltpu.make_async_copy(relay, relay, across_send.at[0]).wait()
    pltpu.make_async_copy(stat.at[pl.ds(0, 31)], stat.at[pl.ds(0, 31)], stat_sem.at[0]).wait()
    for array in range(3):
        sent = stage.at[array, pl.ds(0, 31 * RUN)]
        pltpu.make_async_copy(sent, sent, back_send.at[array]).wait()
    for array in range(3):
        pltpu.make_async_copy(out_ref.at[array], out_ref.at[array], back_recv.at[array]).wait()


def on_device(queries, keys, values, outputs, grad_out, log_totals, pair_live):
    anywhere = pl.BlockSpec(memory_space=pl.ANY)
    rows = B * BLOCKS
    pairs = 3 * BLOCKS
    flops = 10 * pairs * B * B * HD
    grads = pl.pallas_call(
        functools.partial(kernel, lax.axis_size("ctx")),
        out_shape=pltpu.VMEM((3, *queries.shape), jnp.bfloat16),
        in_specs=[
            pl.BlockSpec(memory_space=pltpu.SMEM),
            anywhere,
            anywhere,
            anywhere,
            anywhere,
            anywhere,
            anywhere,
        ],
        out_specs=anywhere,
        scratch_shapes=[
            pltpu.VMEM((4, rows, HD), jnp.bfloat16),
            pltpu.VMEM((2, RUN, 8 * HD), jnp.bfloat16),
            pltpu.VMEM((BLOCKS * RUNS, 2, HD), jnp.float32),
            pltpu.VMEM((H, 2, HD), jnp.float32),
            pltpu.VMEM((pairs, B, B), jnp.float32),
            pltpu.VMEM((pairs, B, B), jnp.bfloat16),
            pltpu.VMEM((3, rows, HD), jnp.bfloat16),
            pltpu.VMEM((2, RUN, H * HD), jnp.bfloat16),
            pltpu.VMEM((H, RUN), jnp.float32),
            pltpu.SemaphoreType.DMA((3,)),
            pltpu.SemaphoreType.DMA((4,)),
            pltpu.SemaphoreType.DMA((4,)),
            pltpu.SemaphoreType.DMA((1,)),
            pltpu.SemaphoreType.DMA((2,)),
            pltpu.SemaphoreType.DMA((2,)),
            pltpu.SemaphoreType.DMA((3,)),
            pltpu.SemaphoreType.DMA((3,)),
        ],
        compiler_params=pltpu.CompilerParams(
            collective_id=0, has_side_effects=True, vmem_limit_bytes=56 * 1024 * 1024
        ),
        cost_estimate=pl.CostEstimate(
            flops=flops, bytes_accessed=8 * RUN * H * HD * 2, transcendentals=pairs * B * B
        ),
        name="pair_attention_backward",
    )(
        pair_live,
        *(
            pltpu.with_memory_space_constraint(array, pltpu.HBM)
            for array in (jnp.transpose(log_totals), queries, keys, values, outputs, grad_out)
        ),
    )
    return grads[0], grads[1], grads[2]


def solution(mesh):
    rows = P(("head", "ctx"), None)
    return jax.shard_map(
        on_device,
        mesh=mesh,
        in_specs=(rows, rows, rows, rows, rows, rows, P()),
        out_specs=(rows, rows, rows),
        check_vma=False,
    )
```

```python
import functools

import jax
import jax.numpy as jnp
from jax import lax
from jax.experimental import pallas as pl
from jax.experimental.pallas import tpu as pltpu
from jax.sharding import PartitionSpec as P

H = 32
HD = 128
RUN = 64
RUNS = 8
BLOCKS = 4
B = RUN * RUNS
LOG2E = 1.4426950408889634
SCALE = 1.0 / HD**0.5
Q, K, DO, V = 0, 1, 2, 3
NT = (((1,), (1,)), ((), ()))
NN = (((1,), (0,)), ((), ()))
TN = (((0,), (0,)), ((), ()))


def dot(a, b, dims):
    return lax.dot_general(a, b, dims, preferred_element_type=jnp.float32)


def partner(block, step):
    if step == 0:
        return block
    if step == 1:
        return block + 1 - 2 * (block % 2)
    return (block + 2) % 4


def kernel(
    ctx_size,
    live_ref,
    lse_ref,
    q_ref,
    k_ref,
    v_ref,
    o_ref,
    do_ref,
    out_ref,
    buf,
    stat,
    stat_src,
    probs,
    grad_s,
    stage,
    rows,
    lse_rows,
    load_sem,
    send_sem,
    recv_sem,
    stat_sem,
    back_send,
    back_recv,
):
    run = lax.axis_index("head")
    ctx = lax.axis_index("ctx")
    quarter = ctx_size // 4
    rest = ctx % quarter
    y_lo = ctx // quarter // 2
    z_hi = ctx // quarter % 2
    y = run // 2 * 2 + y_lo
    core = run % 2
    block = z_hi * 2 + y_lo

    def head(z_there, core_there, y_there):
        return z_there * 16 + core_there * 8 + y_there

    def columns(index):
        return pl.ds(pl.multiple_of(index * HD, HD), HD)

    def device(y_there, core_there, z_there):
        ctx_there = (y_there % 2 * 2 + z_there) * quarter + rest
        return (y_there // 2 * 2 + core_there, ctx_there)

    def send(source, target, sent, received, where):
        pltpu.make_async_remote_copy(
            src_ref=source,
            dst_ref=target,
            send_sem=sent,
            recv_sem=received,
            device_id=where,
            device_id_type=pl.DeviceIdType.MESH,
        ).start()

    def y_at(p):
        return (y + 4 + (p % 2) * ((p + 1) // 2) - (1 - p % 2) * (p // 2)) % 8

    def each(first, last, body):
        lax.fori_loop(first, last, lambda t, carry: (body(t), carry)[1], 0)

    def peer(t):
        return (core + 1 - t % 2) % 2, y_at(t // 4), (z_hi + 1 - t // 2 % 2) % 2

    barrier = pltpu.get_barrier_semaphore()

    def greet(where):
        pl.semaphore_signal(barrier, inc=1, device_id=where, device_id_type=pl.DeviceIdType.MESH)

    def greet_peer(t):
        core_there, y_there, z_there = peer(t)
        greet(device(y_there, core_there, z_there))

    each(0, 31, greet_peer)
    load_do = pltpu.make_async_copy(do_ref, rows.at[0], load_sem.at[0])
    load_o = pltpu.make_async_copy(o_ref, rows.at[1], load_sem.at[1])
    load_lse = pltpu.make_async_copy(lse_ref, lse_rows, load_sem.at[2])
    load_do.start()
    load_o.start()
    load_lse.start()
    pl.semaphore_wait(barrier, 31)

    def slot(array):
        return buf.at[array, pl.ds(pl.multiple_of((block * RUNS + run) * RUN, RUN), RUN)]

    def send_rows(source, array):
        def body(t):
            core_there, y_there, z_there = peer(t)
            send(
                source.at[:, columns(head(z_there, core_there, y_there))],
                slot(array),
                send_sem.at[array],
                recv_sem.at[array],
                device(y_there, core_there, z_there),
            )

        mine = source.at[:, columns(head(z_hi, core, y))]
        pltpu.make_async_copy(mine, slot(array), recv_sem.at[array]).start()
        each(0, 31, body)

    send_rows(q_ref, Q)
    send_rows(k_ref, K)

    load_do.wait()
    load_o.wait()
    load_lse.wait()
    lanes = lax.broadcasted_iota(jnp.int32, (8, HD), 1)
    half = jnp.where(lanes // RUN == run % 2, 1.0, 0.0).astype(jnp.float32)
    twice = jnp.where(
        lax.broadcasted_iota(jnp.int32, (RUN, HD), 0) == lax.broadcasted_iota(jnp.int32, (RUN, HD), 1) % RUN, 1.0, 0.0
    ).astype(jnp.float32)
    lse_lines = lax.dot_general(
        lse_rows[...], twice, NN, precision=lax.Precision.HIGHEST, preferred_element_type=jnp.float32
    )
    stat_src[:, 0, :] = lse_lines * half[:1]
    ones = jnp.ones((8, 2 * HD), jnp.bfloat16)

    def delta_line(h):
        product = rows[0, :, columns(h)].astype(jnp.float32) * rows[1, :, columns(h)].astype(jnp.float32)
        high = product.astype(jnp.bfloat16)
        low = (product - high.astype(jnp.float32)).astype(jnp.bfloat16)
        both = jnp.concatenate([high, low], axis=1)
        line = dot(ones, jnp.concatenate([both, both], axis=0), NT) * half
        stat_src[h, 1:2, :] = line[:1]

    each(0, H, delta_line)

    def send_stat(t):
        core_there, y_there, z_there = peer(t)
        send(
            stat_src.at[head(z_there, core_there, y_there)],
            stat.at[block * RUNS + run],
            stat_sem.at[0],
            stat_sem.at[1],
            device(y_there, core_there, z_there),
        )

    pltpu.make_async_copy(stat_src.at[head(z_hi, core, y)], stat.at[block * RUNS + run], stat_sem.at[1]).start()
    each(0, 31, send_stat)
    send_rows(do_ref, DO)
    send_rows(v_ref, V)

    def arrived(array):
        pltpu.make_async_copy(buf.at[array], buf.at[array], recv_sem.at[array]).wait()

    def rows_of(array, index):
        return buf[array, pl.ds(pl.multiple_of(index * B, B), B), :]

    def stat_line(index, which):
        parts = []
        for pair in range(RUNS // 2):
            parts.append(
                stat[index * RUNS + 2 * pair, which : which + 1, :]
                + stat[index * RUNS + 2 * pair + 1, which : which + 1, :]
            )
        return jnp.concatenate(parts, axis=1)

    arrived(Q)
    arrived(K)
    pltpu.make_async_copy(stat, stat, stat_sem.at[1]).wait()

    def probs_of(i):
        line = stat_line(i, 0) * LOG2E
        queries = rows_of(Q, i)
        ctx_i = (i % 2 * 2 + i // 2) * quarter + rest
        for step in range(3):
            offset = line
            if step > 0:
                dead = (1 - live_ref[step - 1, ctx_i]).astype(jnp.float32)
                offset = line + dead * 1e30
            keys = rows_of(K, partner(i, step))
            scores = dot(keys, queries, NT) * (SCALE * LOG2E)
            probs[i * 3 + step] = jnp.exp2(scores - offset)

    each(0, BLOCKS, probs_of)

    def staged(array, index):
        return stage.at[array, pl.ds(pl.multiple_of(index * B, B), B)]

    def staged_run(array, index, run_there):
        return stage.at[array, pl.ds(pl.multiple_of((index * RUNS + run_there) * RUN, RUN), RUN)]

    def give_back(array, result_of):
        target = out_ref.at[array, :, columns(head(z_hi, core, y))]

        def one_block(t):
            z_there = (z_hi + 1 - t % 2) % 2
            odd = 1 - t // 2
            index = z_there * 2 + (y_lo + odd) % 2
            staged(array, index)[...] = result_of(index).astype(jnp.bfloat16)

            def body(u):
                q = u // 2
                y_there = y_at(4 * (q // 2) + (q % 2) * (3 - 2 * odd) + odd)
                core_there = (core + 1 - u % 2) % 2
                send(
                    staged_run(array, index, y_there // 2 * 2 + core_there),
                    target,
                    back_send.at[array],
                    back_recv.at[array],
                    device(y_there, core_there, z_there),
                )

            each(0, 8 - t // 3, body)

        each(0, BLOCKS, one_block)
        pltpu.make_async_copy(staged_run(array, block, run), target, back_recv.at[array]).start()

    arrived(DO)

    def grad_v_of(j):
        total = jnp.zeros((B, HD), jnp.float32)
        for step in range(3):
            i = partner(j, step)
            total += dot(probs[i * 3 + step].astype(jnp.bfloat16), rows_of(DO, i), NN)
        return total

    give_back(2, grad_v_of)
    arrived(V)

    def grad_k_of(j):
        total = jnp.zeros((B, HD), jnp.float32)
        values = rows_of(V, j)
        for step in range(3):
            i = partner(j, step)
            grad_p = dot(values, rows_of(DO, i), NT)
            grad = (probs[i * 3 + step] * (grad_p - stat_line(i, 1))).astype(jnp.bfloat16)
            grad_s[i * 3 + step] = grad
            total += dot(grad, rows_of(Q, i), NN)
        return total * SCALE

    give_back(1, grad_k_of)

    def grad_q_of(i):
        total = jnp.zeros((B, HD), jnp.float32)
        for step in range(3):
            total += dot(grad_s[i * 3 + step], rows_of(K, partner(i, step)), TN)
        return total * SCALE

    give_back(0, grad_q_of)

    for array in range(4):
        sent = buf.at[array, pl.ds(0, 31 * RUN)]
        pltpu.make_async_copy(sent, sent, send_sem.at[array]).wait()
    pltpu.make_async_copy(stat.at[pl.ds(0, 31)], stat.at[pl.ds(0, 31)], stat_sem.at[0]).wait()
    for array in range(3):
        sent = stage.at[array, pl.ds(0, 31 * RUN)]
        pltpu.make_async_copy(sent, sent, back_send.at[array]).wait()
    for array in range(3):
        pltpu.make_async_copy(out_ref.at[array], out_ref.at[array], back_recv.at[array]).wait()


def on_device(queries, keys, values, outputs, grad_out, log_totals, pair_live):
    anywhere = pl.BlockSpec(memory_space=pl.ANY)
    rows = B * BLOCKS
    pairs = 3 * BLOCKS
    flops = 10 * pairs * B * B * HD
    grads = pl.pallas_call(
        functools.partial(kernel, lax.axis_size("ctx")),
        out_shape=pltpu.VMEM((3, *queries.shape), jnp.bfloat16),
        in_specs=[
            pl.BlockSpec(memory_space=pltpu.SMEM),
            anywhere,
            anywhere,
            anywhere,
            anywhere,
            anywhere,
            anywhere,
        ],
        out_specs=anywhere,
        scratch_shapes=[
            pltpu.VMEM((4, rows, HD), jnp.bfloat16),
            pltpu.VMEM((BLOCKS * RUNS, 2, HD), jnp.float32),
            pltpu.VMEM((H, 2, HD), jnp.float32),
            pltpu.VMEM((pairs, B, B), jnp.float32),
            pltpu.VMEM((pairs, B, B), jnp.bfloat16),
            pltpu.VMEM((3, rows, HD), jnp.bfloat16),
            pltpu.VMEM((2, RUN, H * HD), jnp.bfloat16),
            pltpu.VMEM((H, RUN), jnp.float32),
            pltpu.SemaphoreType.DMA((3,)),
            pltpu.SemaphoreType.DMA((4,)),
            pltpu.SemaphoreType.DMA((4,)),
            pltpu.SemaphoreType.DMA((2,)),
            pltpu.SemaphoreType.DMA((3,)),
            pltpu.SemaphoreType.DMA((3,)),
        ],
        compiler_params=pltpu.CompilerParams(
            collective_id=0, has_side_effects=True, vmem_limit_bytes=56 * 1024 * 1024
        ),
        cost_estimate=pl.CostEstimate(
            flops=flops, bytes_accessed=8 * RUN * H * HD * 2, transcendentals=pairs * B * B
        ),
        name="pair_attention_backward",
    )(
        pair_live,
        *(
            pltpu.with_memory_space_constraint(array, pltpu.HBM)
            for array in (jnp.transpose(log_totals), queries, keys, values, outputs, grad_out)
        ),
    )
    return grads[0], grads[1], grads[2]


def solution(mesh):
    rows = P(("head", "ctx"), None)
    return jax.shard_map(
        on_device,
        mesh=mesh,
        in_specs=(rows, rows, rows, rows, rows, rows, P()),
        out_specs=(rows, rows, rows),
        check_vma=False,
    )
```

```python
import functools

import jax
import jax.numpy as jnp
from jax import lax
from jax.experimental import pallas as pl
from jax.experimental.pallas import tpu as pltpu
from jax.sharding import PartitionSpec as P

H = 32
HD = 128
RUN = 64
RUNS = 8
BLOCKS = 4
B = RUN * RUNS
LOG2E = 1.4426950408889634
SCALE = 1.0 / HD**0.5
Q, K, DO, V = 0, 1, 2, 3
NT = (((1,), (1,)), ((), ()))
NN = (((1,), (0,)), ((), ()))
TN = (((0,), (0,)), ((), ()))


def dot(a, b, dims):
    return lax.dot_general(a, b, dims, preferred_element_type=jnp.float32)


def partner(block, step):
    if step == 0:
        return block
    if step == 1:
        return block + 1 - 2 * (block % 2)
    return (block + 2) % 4


def kernel(
    ctx_size,
    live_ref,
    lse_ref,
    q_ref,
    k_ref,
    v_ref,
    o_ref,
    do_ref,
    out_ref,
    buf,
    stat,
    stat_src,
    probs,
    grad_s,
    stage,
    rows,
    lse_rows,
    load_sem,
    send_sem,
    recv_sem,
    stat_sem,
    column_sem,
    back_send,
    back_recv,
):
    run = lax.axis_index("head")
    ctx = lax.axis_index("ctx")
    quarter = ctx_size // 4
    rest = ctx % quarter
    y_lo = ctx // quarter // 2
    z_hi = ctx // quarter % 2
    y = run // 2 * 2 + y_lo
    core = run % 2
    block = z_hi * 2 + y_lo

    def head(z_there, core_there, y_there):
        return z_there * 16 + core_there * 8 + y_there

    def columns(index):
        return pl.ds(pl.multiple_of(index * HD, HD), HD)

    def device(y_there, core_there, z_there):
        ctx_there = (y_there % 2 * 2 + z_there) * quarter + rest
        return (y_there // 2 * 2 + core_there, ctx_there)

    def send(source, target, sent, received, where):
        pltpu.make_async_remote_copy(
            src_ref=source,
            dst_ref=target,
            send_sem=sent,
            recv_sem=received,
            device_id=where,
            device_id_type=pl.DeviceIdType.MESH,
        ).start()

    def y_at(p):
        return (y + 4 + (p % 2) * ((p + 1) // 2) - (1 - p % 2) * (p // 2)) % 8

    def each(first, last, body):
        lax.fori_loop(first, last, lambda t, carry: (body(t), carry)[1], 0)

    def peer(t):
        return (core + 1 - t % 2) % 2, y_at(t // 4), (z_hi + 1 - t // 2 % 2) % 2

    barrier = pltpu.get_barrier_semaphore()

    def greet(where):
        pl.semaphore_signal(barrier, inc=1, device_id=where, device_id_type=pl.DeviceIdType.MESH)

    def column_peer(t):
        near = t // 15
        return (core + 1 - (t + near) % 2) % 2, y_at(t // 2 - near * (t // 2 - 7)), (z_hi + near) % 2

    def partners_peer(t):
        return (core + 1 - t % 2) % 2, y_at(t // 2), 1 - z_hi

    def greet_peer(t):
        core_there, y_there, z_there = column_peer(t)
        greet(device(y_there, core_there, z_there))

    each(0, 17, greet_peer)
    load_do = pltpu.make_async_copy(do_ref, rows.at[0], load_sem.at[0])
    load_o = pltpu.make_async_copy(o_ref, rows.at[1], load_sem.at[1])
    load_lse = pltpu.make_async_copy(lse_ref, lse_rows, load_sem.at[2])
    load_do.start()
    load_o.start()
    load_lse.start()
    pl.semaphore_wait(barrier, 17)
    pl.semaphore_signal(
        column_sem, inc=1, device_id=device(y, core, 1 - z_hi), device_id_type=pl.DeviceIdType.MESH
    )

    def slot(array):
        return buf.at[array, pl.ds(pl.multiple_of((block * RUNS + run) * RUN, RUN), RUN)]

    def send_rows(source, array, peers, count):
        def body(t):
            core_there, y_there, z_there = peers(t)
            send(
                source.at[:, columns(head(z_there, core_there, y_there))],
                slot(array),
                send_sem.at[array],
                recv_sem.at[array],
                device(y_there, core_there, z_there),
            )

        each(0, count, body)

    def keep_rows(source, array):
        mine = source.at[:, columns(head(z_hi, core, y))]
        pltpu.make_async_copy(mine, slot(array), recv_sem.at[array]).start()

    send_rows(q_ref, Q, column_peer, 17)
    send_rows(k_ref, K, column_peer, 17)
    for array, source in ((Q, q_ref), (K, k_ref), (DO, do_ref), (V, v_ref)):
        keep_rows(source, array)
    pl.semaphore_wait(column_sem, 1)
    send_rows(q_ref, Q, partners_peer, 14)
    send_rows(k_ref, K, partners_peer, 14)

    load_do.wait()
    load_o.wait()
    load_lse.wait()
    lanes = lax.broadcasted_iota(jnp.int32, (8, HD), 1)
    half = jnp.where(lanes // RUN == run % 2, 1.0, 0.0).astype(jnp.float32)
    twice = jnp.where(
        lax.broadcasted_iota(jnp.int32, (RUN, HD), 0) == lax.broadcasted_iota(jnp.int32, (RUN, HD), 1) % RUN, 1.0, 0.0
    ).astype(jnp.float32)
    lse_lines = lax.dot_general(
        lse_rows[...], twice, NN, precision=lax.Precision.HIGHEST, preferred_element_type=jnp.float32
    )
    stat_src[:, 0, :] = lse_lines * half[:1]
    ones = jnp.ones((8, 2 * HD), jnp.bfloat16)

    def delta_line(h):
        product = rows[0, :, columns(h)].astype(jnp.float32) * rows[1, :, columns(h)].astype(jnp.float32)
        high = product.astype(jnp.bfloat16)
        low = (product - high.astype(jnp.float32)).astype(jnp.bfloat16)
        both = jnp.concatenate([high, low], axis=1)
        line = dot(ones, jnp.concatenate([both, both], axis=0), NT) * half
        stat_src[h, 1:2, :] = line[:1]

    each(0, H, delta_line)

    def send_stat(t):
        core_there, y_there, z_there = peer(t)
        send(
            stat_src.at[head(z_there, core_there, y_there)],
            stat.at[block * RUNS + run],
            stat_sem.at[0],
            stat_sem.at[1],
            device(y_there, core_there, z_there),
        )

    pltpu.make_async_copy(stat_src.at[head(z_hi, core, y)], stat.at[block * RUNS + run], stat_sem.at[1]).start()
    each(0, 31, send_stat)
    send_rows(do_ref, DO, peer, 31)
    send_rows(v_ref, V, peer, 31)

    def arrived(array):
        pltpu.make_async_copy(buf.at[array], buf.at[array], recv_sem.at[array]).wait()

    def rows_of(array, index):
        return buf[array, pl.ds(pl.multiple_of(index * B, B), B), :]

    def stat_line(index, which):
        parts = []
        for pair in range(RUNS // 2):
            parts.append(
                stat[index * RUNS + 2 * pair, which : which + 1, :]
                + stat[index * RUNS + 2 * pair + 1, which : which + 1, :]
            )
        return jnp.concatenate(parts, axis=1)

    arrived(Q)
    arrived(K)
    pltpu.make_async_copy(stat, stat, stat_sem.at[1]).wait()

    def probs_of(i):
        line = stat_line(i, 0) * LOG2E
        queries = rows_of(Q, i)
        ctx_i = (i % 2 * 2 + i // 2) * quarter + rest
        for step in range(3):
            offset = line
            if step > 0:
                dead = (1 - live_ref[step - 1, ctx_i]).astype(jnp.float32)
                offset = line + dead * 1e30
            keys = rows_of(K, partner(i, step))
            scores = dot(keys, queries, NT) * (SCALE * LOG2E)
            probs[i * 3 + step] = jnp.exp2(scores - offset)

    each(0, BLOCKS, probs_of)

    def staged(array, index):
        return stage.at[array, pl.ds(pl.multiple_of(index * B, B), B)]

    def staged_run(array, index, run_there):
        return stage.at[array, pl.ds(pl.multiple_of((index * RUNS + run_there) * RUN, RUN), RUN)]

    def give_back(array, result_of):
        target = out_ref.at[array, :, columns(head(z_hi, core, y))]

        def one_block(t):
            z_there = (z_hi + 1 - t % 2) % 2
            odd = 1 - t // 2
            index = z_there * 2 + (y_lo + odd) % 2
            staged(array, index)[...] = result_of(index).astype(jnp.bfloat16)

            def body(u):
                q = u // 2
                y_there = y_at(4 * (q // 2) + (q % 2) * (3 - 2 * odd) + odd)
                core_there = (core + 1 - u % 2) % 2
                send(
                    staged_run(array, index, y_there // 2 * 2 + core_there),
                    target,
                    back_send.at[array],
                    back_recv.at[array],
                    device(y_there, core_there, z_there),
                )

            each(0, 8 - t // 3, body)

        each(0, BLOCKS, one_block)
        pltpu.make_async_copy(staged_run(array, block, run), target, back_recv.at[array]).start()

    arrived(DO)

    def grad_v_of(j):
        total = jnp.zeros((B, HD), jnp.float32)
        for step in range(3):
            i = partner(j, step)
            total += dot(probs[i * 3 + step].astype(jnp.bfloat16), rows_of(DO, i), NN)
        return total

    give_back(2, grad_v_of)
    arrived(V)

    def grad_k_of(j):
        total = jnp.zeros((B, HD), jnp.float32)
        values = rows_of(V, j)
        for step in range(3):
            i = partner(j, step)
            grad_p = dot(values, rows_of(DO, i), NT)
            grad = (probs[i * 3 + step] * (grad_p - stat_line(i, 1))).astype(jnp.bfloat16)
            grad_s[i * 3 + step] = grad
            total += dot(grad, rows_of(Q, i), NN)
        return total * SCALE

    give_back(1, grad_k_of)

    def grad_q_of(i):
        total = jnp.zeros((B, HD), jnp.float32)
        for step in range(3):
            total += dot(grad_s[i * 3 + step], rows_of(K, partner(i, step)), TN)
        return total * SCALE

    give_back(0, grad_q_of)

    for array in range(4):
        sent = buf.at[array, pl.ds(0, 31 * RUN)]
        pltpu.make_async_copy(sent, sent, send_sem.at[array]).wait()
    pltpu.make_async_copy(stat.at[pl.ds(0, 31)], stat.at[pl.ds(0, 31)], stat_sem.at[0]).wait()
    for array in range(3):
        sent = stage.at[array, pl.ds(0, 31 * RUN)]
        pltpu.make_async_copy(sent, sent, back_send.at[array]).wait()
    for array in range(3):
        pltpu.make_async_copy(out_ref.at[array], out_ref.at[array], back_recv.at[array]).wait()


def on_device(queries, keys, values, outputs, grad_out, log_totals, pair_live):
    anywhere = pl.BlockSpec(memory_space=pl.ANY)
    rows = B * BLOCKS
    pairs = 3 * BLOCKS
    flops = 10 * pairs * B * B * HD
    grads = pl.pallas_call(
        functools.partial(kernel, lax.axis_size("ctx")),
        out_shape=pltpu.VMEM((3, *queries.shape), jnp.bfloat16),
        in_specs=[
            pl.BlockSpec(memory_space=pltpu.SMEM),
            anywhere,
            anywhere,
            anywhere,
            anywhere,
            anywhere,
            anywhere,
        ],
        out_specs=anywhere,
        scratch_shapes=[
            pltpu.VMEM((4, rows, HD), jnp.bfloat16),
            pltpu.VMEM((BLOCKS * RUNS, 2, HD), jnp.float32),
            pltpu.VMEM((H, 2, HD), jnp.float32),
            pltpu.VMEM((pairs, B, B), jnp.float32),
            pltpu.VMEM((pairs, B, B), jnp.bfloat16),
            pltpu.VMEM((3, rows, HD), jnp.bfloat16),
            pltpu.VMEM((2, RUN, H * HD), jnp.bfloat16),
            pltpu.VMEM((H, RUN), jnp.float32),
            pltpu.SemaphoreType.DMA((3,)),
            pltpu.SemaphoreType.DMA((4,)),
            pltpu.SemaphoreType.DMA((4,)),
            pltpu.SemaphoreType.DMA((2,)),
            pltpu.SemaphoreType.REGULAR,
            pltpu.SemaphoreType.DMA((3,)),
            pltpu.SemaphoreType.DMA((3,)),
        ],
        compiler_params=pltpu.CompilerParams(
            collective_id=0, has_side_effects=True, vmem_limit_bytes=56 * 1024 * 1024
        ),
        cost_estimate=pl.CostEstimate(
            flops=flops, bytes_accessed=8 * RUN * H * HD * 2, transcendentals=pairs * B * B
        ),
        name="pair_attention_backward",
    )(
        pair_live,
        *(
            pltpu.with_memory_space_constraint(array, pltpu.HBM)
            for array in (jnp.transpose(log_totals), queries, keys, values, outputs, grad_out)
        ),
    )
    return grads[0], grads[1], grads[2]


def solution(mesh):
    rows = P(("head", "ctx"), None)
    return jax.shard_map(
        on_device,
        mesh=mesh,
        in_specs=(rows, rows, rows, rows, rows, rows, P()),
        out_specs=(rows, rows, rows),
        check_vma=False,
    )
```

```python
import functools

import jax
import jax.numpy as jnp
from jax import lax
from jax.experimental import pallas as pl
from jax.experimental.pallas import tpu as pltpu
from jax.sharding import PartitionSpec as P

H = 32
HD = 128
RUN = 64
RUNS = 8
BLOCKS = 4
B = RUN * RUNS
LOG2E = 1.4426950408889634
SCALE = 1.0 / HD**0.5
Q, K, DO, V = 0, 1, 2, 3
NT = (((1,), (1,)), ((), ()))
NN = (((1,), (0,)), ((), ()))
TN = (((0,), (0,)), ((), ()))


def dot(a, b, dims):
    return lax.dot_general(a, b, dims, preferred_element_type=jnp.float32)


def partner(block, step):
    if step == 0:
        return block
    if step == 1:
        return block + 1 - 2 * (block % 2)
    return (block + 2) % 4


def kernel(
    ctx_size,
    live_ref,
    lse_ref,
    q_ref,
    k_ref,
    v_ref,
    o_ref,
    do_ref,
    out_ref,
    buf,
    stat,
    stat_src,
    probs,
    grad_s,
    stage,
    rows,
    lse_rows,
    load_sem,
    send_sem,
    recv_sem,
    stat_sem,
    back_send,
    back_recv,
):
    run = lax.axis_index("head")
    ctx = lax.axis_index("ctx")
    quarter = ctx_size // 4
    rest = ctx % quarter
    y_lo = ctx // quarter // 2
    z_hi = ctx // quarter % 2
    y = run // 2 * 2 + y_lo
    core = run % 2
    block = z_hi * 2 + y_lo

    def head(z_there, core_there, y_there):
        return z_there * 16 + core_there * 8 + y_there

    def columns(index):
        return pl.ds(pl.multiple_of(index * HD, HD), HD)

    def device(y_there, core_there, z_there):
        ctx_there = (y_there % 2 * 2 + z_there) * quarter + rest
        return (y_there // 2 * 2 + core_there, ctx_there)

    def send(source, target, sent, received, where):
        pltpu.make_async_remote_copy(
            src_ref=source,
            dst_ref=target,
            send_sem=sent,
            recv_sem=received,
            device_id=where,
            device_id_type=pl.DeviceIdType.MESH,
        ).start()

    def y_at(p):
        i = p // 2
        return (y + 4 + i - i // 2 * (2 * i - 1) + 4 * (p % 2)) % 8

    def each(first, last, body):
        lax.fori_loop(first, last, lambda t, carry: (body(t), carry)[1], 0)

    def place(t):
        return (core + 1 - t % 2) % 2, y_at(t // 4), (z_hi + 1 - t // 2 % 2) % 2

    def peer(t):
        return place(t + (t + 24) // 31)

    barrier = pltpu.get_barrier_semaphore()

    def greet(where):
        pl.semaphore_signal(barrier, inc=1, device_id=where, device_id_type=pl.DeviceIdType.MESH)

    def greet_peer(t):
        core_there, y_there, z_there = peer(t)
        greet(device(y_there, core_there, z_there))

    each(0, 31, greet_peer)
    load_do = pltpu.make_async_copy(do_ref, rows.at[0], load_sem.at[0])
    load_o = pltpu.make_async_copy(o_ref, rows.at[1], load_sem.at[1])
    load_lse = pltpu.make_async_copy(lse_ref, lse_rows, load_sem.at[2])
    load_do.start()
    load_o.start()
    load_lse.start()
    pl.semaphore_wait(barrier, 31)

    def slot(array):
        return buf.at[array, pl.ds(pl.multiple_of((block * RUNS + run) * RUN, RUN), RUN)]

    def send_rows(source, array):
        def body(t):
            core_there, y_there, z_there = peer(t)
            send(
                source.at[:, columns(head(z_there, core_there, y_there))],
                slot(array),
                send_sem.at[array],
                recv_sem.at[array],
                device(y_there, core_there, z_there),
            )

        mine = source.at[:, columns(head(z_hi, core, y))]
        pltpu.make_async_copy(mine, slot(array), recv_sem.at[array]).start()
        each(0, 31, body)

    send_rows(q_ref, Q)
    send_rows(k_ref, K)

    load_do.wait()
    load_o.wait()
    load_lse.wait()
    lanes = lax.broadcasted_iota(jnp.int32, (8, HD), 1)
    half = jnp.where(lanes // RUN == run % 2, 1.0, 0.0).astype(jnp.float32)
    twice = jnp.where(
        lax.broadcasted_iota(jnp.int32, (RUN, HD), 0) == lax.broadcasted_iota(jnp.int32, (RUN, HD), 1) % RUN, 1.0, 0.0
    ).astype(jnp.float32)
    lse_lines = lax.dot_general(
        lse_rows[...], twice, NN, precision=lax.Precision.HIGHEST, preferred_element_type=jnp.float32
    )
    stat_src[:, 0, :] = lse_lines * half[:1]
    ones = jnp.ones((8, 2 * HD), jnp.bfloat16)

    def delta_line(h):
        product = rows[0, :, columns(h)].astype(jnp.float32) * rows[1, :, columns(h)].astype(jnp.float32)
        high = product.astype(jnp.bfloat16)
        low = (product - high.astype(jnp.float32)).astype(jnp.bfloat16)
        both = jnp.concatenate([high, low], axis=1)
        line = dot(ones, jnp.concatenate([both, both], axis=0), NT) * half
        stat_src[h, 1:2, :] = line[:1]

    each(0, H, delta_line)

    def send_stat(t):
        core_there, y_there, z_there = peer(t)
        send(
            stat_src.at[head(z_there, core_there, y_there)],
            stat.at[block * RUNS + run],
            stat_sem.at[0],
            stat_sem.at[1],
            device(y_there, core_there, z_there),
        )

    pltpu.make_async_copy(stat_src.at[head(z_hi, core, y)], stat.at[block * RUNS + run], stat_sem.at[1]).start()
    each(0, 31, send_stat)
    send_rows(do_ref, DO)
    send_rows(v_ref, V)

    def arrived(array):
        pltpu.make_async_copy(buf.at[array], buf.at[array], recv_sem.at[array]).wait()

    def rows_of(array, index):
        return buf[array, pl.ds(pl.multiple_of(index * B, B), B), :]

    def stat_line(index, which):
        parts = []
        for pair in range(RUNS // 2):
            parts.append(
                stat[index * RUNS + 2 * pair, which : which + 1, :]
                + stat[index * RUNS + 2 * pair + 1, which : which + 1, :]
            )
        return jnp.concatenate(parts, axis=1)

    arrived(Q)
    arrived(K)
    pltpu.make_async_copy(stat, stat, stat_sem.at[1]).wait()

    def probs_of(i):
        line = stat_line(i, 0) * LOG2E
        queries = rows_of(Q, i)
        ctx_i = (i % 2 * 2 + i // 2) * quarter + rest
        for step in range(3):
            offset = line
            if step > 0:
                dead = (1 - live_ref[step - 1, ctx_i]).astype(jnp.float32)
                offset = line + dead * 1e30
            keys = rows_of(K, partner(i, step))
            scores = dot(keys, queries, NT) * (SCALE * LOG2E)
            probs[i * 3 + step] = jnp.exp2(scores - offset)

    each(0, BLOCKS, probs_of)

    def staged(array, index):
        return stage.at[array, pl.ds(pl.multiple_of(index * B, B), B)]

    def staged_run(array, index, run_there):
        return stage.at[array, pl.ds(pl.multiple_of((index * RUNS + run_there) * RUN, RUN), RUN)]

    def give_back(array, result_of):
        target = out_ref.at[array, :, columns(head(z_hi, core, y))]

        def half_of_blocks(t):
            odd = 1 - t
            y_there_lo = (y_lo + odd) % 2

            def one_block(z):
                staged(array, z * 2 + y_there_lo)[...] = result_of(z * 2 + y_there_lo).astype(jnp.bfloat16)

            each(0, 2, one_block)

            def body(u):
                v = u + t * ((u + 24) // 31)
                q = v // 4
                core_there, y_there, z_there = place(4 * (q + 2 * odd + t * 4 * (q // 2)) + v % 4)
                send(
                    staged_run(array, z_there * 2 + y_there_lo, y_there // 2 * 2 + core_there),
                    target,
                    back_send.at[array],
                    back_recv.at[array],
                    device(y_there, core_there, z_there),
                )

            each(0, 16 - t, body)

        each(0, 2, half_of_blocks)
        pltpu.make_async_copy(staged_run(array, block, run), target, back_recv.at[array]).start()

    arrived(DO)

    def grad_v_of(j):
        total = jnp.zeros((B, HD), jnp.float32)
        for step in range(3):
            i = partner(j, step)
            total += dot(probs[i * 3 + step].astype(jnp.bfloat16), rows_of(DO, i), NN)
        return total

    give_back(2, grad_v_of)
    arrived(V)

    def grad_k_of(j):
        total = jnp.zeros((B, HD), jnp.float32)
        values = rows_of(V, j)
        for step in range(3):
            i = partner(j, step)
            grad_p = dot(values, rows_of(DO, i), NT)
            grad = (probs[i * 3 + step] * (grad_p - stat_line(i, 1))).astype(jnp.bfloat16)
            grad_s[i * 3 + step] = grad
            total += dot(grad, rows_of(Q, i), NN)
        return total * SCALE

    give_back(1, grad_k_of)

    def grad_q_of(i):
        total = jnp.zeros((B, HD), jnp.float32)
        for step in range(3):
            total += dot(grad_s[i * 3 + step], rows_of(K, partner(i, step)), TN)
        return total * SCALE

    give_back(0, grad_q_of)

    for array in range(4):
        sent = buf.at[array, pl.ds(0, 31 * RUN)]
        pltpu.make_async_copy(sent, sent, send_sem.at[array]).wait()
    pltpu.make_async_copy(stat.at[pl.ds(0, 31)], stat.at[pl.ds(0, 31)], stat_sem.at[0]).wait()
    for array in range(3):
        sent = stage.at[array, pl.ds(0, 31 * RUN)]
        pltpu.make_async_copy(sent, sent, back_send.at[array]).wait()
    for array in range(3):
        pltpu.make_async_copy(out_ref.at[array], out_ref.at[array], back_recv.at[array]).wait()


def on_device(queries, keys, values, outputs, grad_out, log_totals, pair_live):
    anywhere = pl.BlockSpec(memory_space=pl.ANY)
    rows = B * BLOCKS
    pairs = 3 * BLOCKS
    flops = 10 * pairs * B * B * HD
    grads = pl.pallas_call(
        functools.partial(kernel, lax.axis_size("ctx")),
        out_shape=pltpu.VMEM((3, *queries.shape), jnp.bfloat16),
        in_specs=[
            pl.BlockSpec(memory_space=pltpu.SMEM),
            anywhere,
            anywhere,
            anywhere,
            anywhere,
            anywhere,
            anywhere,
        ],
        out_specs=anywhere,
        scratch_shapes=[
            pltpu.VMEM((4, rows, HD), jnp.bfloat16),
            pltpu.VMEM((BLOCKS * RUNS, 2, HD), jnp.float32),
            pltpu.VMEM((H, 2, HD), jnp.float32),
            pltpu.VMEM((pairs, B, B), jnp.float32),
            pltpu.VMEM((pairs, B, B), jnp.bfloat16),
            pltpu.VMEM((3, rows, HD), jnp.bfloat16),
            pltpu.VMEM((2, RUN, H * HD), jnp.bfloat16),
            pltpu.VMEM((H, RUN), jnp.float32),
            pltpu.SemaphoreType.DMA((3,)),
            pltpu.SemaphoreType.DMA((4,)),
            pltpu.SemaphoreType.DMA((4,)),
            pltpu.SemaphoreType.DMA((2,)),
            pltpu.SemaphoreType.DMA((3,)),
            pltpu.SemaphoreType.DMA((3,)),
        ],
        compiler_params=pltpu.CompilerParams(
            collective_id=0, has_side_effects=True, vmem_limit_bytes=56 * 1024 * 1024
        ),
        cost_estimate=pl.CostEstimate(
            flops=flops, bytes_accessed=8 * RUN * H * HD * 2, transcendentals=pairs * B * B
        ),
        name="pair_attention_backward",
    )(
        pair_live,
        *(
            pltpu.with_memory_space_constraint(array, pltpu.HBM)
            for array in (jnp.transpose(log_totals), queries, keys, values, outputs, grad_out)
        ),
    )
    return grads[0], grads[1], grads[2]


def solution(mesh):
    rows = P(("head", "ctx"), None)
    return jax.shard_map(
        on_device,
        mesh=mesh,
        in_specs=(rows, rows, rows, rows, rows, rows, P()),
        out_specs=(rows, rows, rows),
        check_vma=False,
    )
```

```python
import functools

import jax
import jax.numpy as jnp
from jax import lax
from jax.experimental import pallas as pl
from jax.experimental.pallas import tpu as pltpu
from jax.sharding import PartitionSpec as P

H = 32
HD = 128
RUN = 64
RUNS = 8
BLOCKS = 4
B = RUN * RUNS
LOG2E = 1.4426950408889634
SCALE = 1.0 / HD**0.5
Q, K, DO, V = 0, 1, 2, 3
NT = (((1,), (1,)), ((), ()))
NN = (((1,), (0,)), ((), ()))
TN = (((0,), (0,)), ((), ()))


def dot(a, b, dims):
    return lax.dot_general(a, b, dims, preferred_element_type=jnp.float32)


def partner(block, step):
    if step == 0:
        return block
    if step == 1:
        return block + 1 - 2 * (block % 2)
    return (block + 2) % 4


def kernel(
    ctx_size,
    live_ref,
    lse_ref,
    q_ref,
    k_ref,
    v_ref,
    o_ref,
    do_ref,
    out_ref,
    buf,
    stat,
    stat_src,
    probs,
    grad_s,
    stage,
    rows,
    lse_rows,
    load_sem,
    send_sem,
    recv_sem,
    stat_sem,
    back_send,
    back_recv,
):
    run = lax.axis_index("head")
    ctx = lax.axis_index("ctx")
    quarter = ctx_size // 4
    rest = ctx % quarter
    y_lo = ctx // quarter // 2
    z_hi = ctx // quarter % 2
    y = run // 2 * 2 + y_lo
    core = run % 2
    block = z_hi * 2 + y_lo

    def head(z_there, core_there, y_there):
        return z_there * 16 + core_there * 8 + y_there

    def columns(index):
        return pl.ds(pl.multiple_of(index * HD, HD), HD)

    def device(y_there, core_there, z_there):
        ctx_there = (y_there % 2 * 2 + z_there) * quarter + rest
        return (y_there // 2 * 2 + core_there, ctx_there)

    def send(source, target, sent, received, where):
        pltpu.make_async_remote_copy(
            src_ref=source,
            dst_ref=target,
            send_sem=sent,
            recv_sem=received,
            device_id=where,
            device_id_type=pl.DeviceIdType.MESH,
        ).start()

    def y_at(p):
        i = p // 2
        return (y + 4 + i - i // 2 * (2 * i - 1) + 4 * (p % 2)) % 8

    def each(first, last, body):
        lax.fori_loop(first, last, lambda t, carry: (body(t), carry)[1], 0)

    def place(t):
        return (core + 1 - t % 2) % 2, y_at(t // 4), (z_hi + 1 - t // 2 % 2) % 2

    def peer(t):
        return place(t + (t + 24) // 31)

    barrier = pltpu.get_barrier_semaphore()

    def greet(where):
        pl.semaphore_signal(barrier, inc=1, device_id=where, device_id_type=pl.DeviceIdType.MESH)

    def greet_peer(t):
        core_there, y_there, z_there = peer(t)
        greet(device(y_there, core_there, z_there))

    each(0, 31, greet_peer)
    load_do = pltpu.make_async_copy(do_ref, rows.at[0], load_sem.at[0])
    load_o = pltpu.make_async_copy(o_ref, rows.at[1], load_sem.at[1])
    load_lse = pltpu.make_async_copy(lse_ref, lse_rows, load_sem.at[2])
    load_do.start()
    load_o.start()
    load_lse.start()
    pl.semaphore_wait(barrier, 31)

    def slot(array):
        return buf.at[array, pl.ds(pl.multiple_of((block * RUNS + run) * RUN, RUN), RUN)]

    def send_rows(source, array):
        def body(t):
            core_there, y_there, z_there = peer(t)
            send(
                source.at[:, columns(head(z_there, core_there, y_there))],
                slot(array),
                send_sem.at[array],
                recv_sem.at[array],
                device(y_there, core_there, z_there),
            )

        mine = source.at[:, columns(head(z_hi, core, y))]
        pltpu.make_async_copy(mine, slot(array), recv_sem.at[array]).start()
        each(0, 31, body)

    send_rows(q_ref, Q)
    send_rows(k_ref, K)

    load_do.wait()
    load_o.wait()
    load_lse.wait()
    lanes = lax.broadcasted_iota(jnp.int32, (8, HD), 1)
    half = jnp.where(lanes // RUN == run % 2, 1.0, 0.0).astype(jnp.float32)
    twice = jnp.where(
        lax.broadcasted_iota(jnp.int32, (RUN, HD), 0) == lax.broadcasted_iota(jnp.int32, (RUN, HD), 1) % RUN, 1.0, 0.0
    ).astype(jnp.float32)
    lse_lines = lax.dot_general(
        lse_rows[...], twice, NN, precision=lax.Precision.HIGHEST, preferred_element_type=jnp.float32
    )
    stat_src[:, 0, :] = lse_lines * half[:1]
    ones = jnp.ones((8, 2 * HD), jnp.bfloat16)

    def delta_line(h):
        product = rows[0, :, columns(h)].astype(jnp.float32) * rows[1, :, columns(h)].astype(jnp.float32)
        high = product.astype(jnp.bfloat16)
        low = (product - high.astype(jnp.float32)).astype(jnp.bfloat16)
        both = jnp.concatenate([high, low], axis=1)
        line = dot(ones, jnp.concatenate([both, both], axis=0), NT) * half
        stat_src[h, 1:2, :] = line[:1]

    each(0, H, delta_line)

    def send_stat(t):
        core_there, y_there, z_there = peer(t)
        send(
            stat_src.at[head(z_there, core_there, y_there)],
            stat.at[block * RUNS + run],
            stat_sem.at[0],
            stat_sem.at[1],
            device(y_there, core_there, z_there),
        )

    pltpu.make_async_copy(stat_src.at[head(z_hi, core, y)], stat.at[block * RUNS + run], stat_sem.at[1]).start()
    each(0, 31, send_stat)
    send_rows(do_ref, DO)
    send_rows(v_ref, V)

    def arrived(array):
        pltpu.make_async_copy(buf.at[array], buf.at[array], recv_sem.at[array]).wait()

    def rows_of(array, index):
        return buf[array, pl.ds(pl.multiple_of(index * B, B), B), :]

    def stat_line(index, which):
        parts = []
        for pair in range(RUNS // 2):
            parts.append(
                stat[index * RUNS + 2 * pair, which : which + 1, :]
                + stat[index * RUNS + 2 * pair + 1, which : which + 1, :]
            )
        return jnp.concatenate(parts, axis=1)

    arrived(Q)
    arrived(K)
    pltpu.make_async_copy(stat, stat, stat_sem.at[1]).wait()

    def probs_of(i):
        line = stat_line(i, 0) * LOG2E
        queries = rows_of(Q, i)
        ctx_i = (i % 2 * 2 + i // 2) * quarter + rest
        for step in range(3):
            offset = line
            if step > 0:
                dead = (1 - live_ref[step - 1, ctx_i]).astype(jnp.float32)
                offset = line + dead * 1e30
            keys = rows_of(K, partner(i, step))
            scores = dot(keys, queries, NT) * (SCALE * LOG2E)
            probs[i * 3 + step] = jnp.exp2(scores - offset)

    each(0, BLOCKS, probs_of)

    def staged(array, index):
        return stage.at[array, pl.ds(pl.multiple_of(index * B, B), B)]

    def staged_run(array, index, run_there):
        return stage.at[array, pl.ds(pl.multiple_of((index * RUNS + run_there) * RUN, RUN), RUN)]

    def give_back(array, result_of):
        target = out_ref.at[array, :, columns(head(z_hi, core, y))]

        def half_of_blocks(t):
            odd = 1 - t
            y_there_lo = (y_lo + odd) % 2

            def one_block(z):
                staged(array, z * 2 + y_there_lo)[...] = result_of(z * 2 + y_there_lo).astype(jnp.bfloat16)

            each(0, 2, one_block)

            def body(u):
                q = u // 4
                q = q + t * ((q + 3) // 4 - 3 * (q // 3))
                core_there, y_there, z_there = place(4 * (q + 2 * odd + t * 4 * (q // 2)) + u % 4)
                send(
                    staged_run(array, z_there * 2 + y_there_lo, y_there // 2 * 2 + core_there),
                    target,
                    back_send.at[array],
                    back_recv.at[array],
                    device(y_there, core_there, z_there),
                )

            each(0, 16 - t, body)

        each(0, 2, half_of_blocks)
        pltpu.make_async_copy(staged_run(array, block, run), target, back_recv.at[array]).start()

    arrived(DO)

    def grad_v_of(j):
        total = jnp.zeros((B, HD), jnp.float32)
        for step in range(3):
            i = partner(j, step)
            total += dot(probs[i * 3 + step].astype(jnp.bfloat16), rows_of(DO, i), NN)
        return total

    give_back(2, grad_v_of)
    arrived(V)

    def grad_k_of(j):
        total = jnp.zeros((B, HD), jnp.float32)
        values = rows_of(V, j)
        for step in range(3):
            i = partner(j, step)
            grad_p = dot(values, rows_of(DO, i), NT)
            grad = (probs[i * 3 + step] * (grad_p - stat_line(i, 1))).astype(jnp.bfloat16)
            grad_s[i * 3 + step] = grad
            total += dot(grad, rows_of(Q, i), NN)
        return total * SCALE

    give_back(1, grad_k_of)

    def grad_q_of(i):
        total = jnp.zeros((B, HD), jnp.float32)
        for step in range(3):
            total += dot(grad_s[i * 3 + step], rows_of(K, partner(i, step)), TN)
        return total * SCALE

    give_back(0, grad_q_of)

    for array in range(4):
        sent = buf.at[array, pl.ds(0, 31 * RUN)]
        pltpu.make_async_copy(sent, sent, send_sem.at[array]).wait()
    pltpu.make_async_copy(stat.at[pl.ds(0, 31)], stat.at[pl.ds(0, 31)], stat_sem.at[0]).wait()
    for array in range(3):
        sent = stage.at[array, pl.ds(0, 31 * RUN)]
        pltpu.make_async_copy(sent, sent, back_send.at[array]).wait()
    for array in range(3):
        pltpu.make_async_copy(out_ref.at[array], out_ref.at[array], back_recv.at[array]).wait()


def store(source, *targets_and_sems):
    *targets, sems = targets_and_sems
    copies = [pltpu.make_async_copy(source.at[i], target, sems.at[i]) for i, target in enumerate(targets)]
    for copy in copies:
        copy.start()
    for copy in copies:
        copy.wait()


def on_device(queries, keys, values, outputs, grad_out, log_totals, pair_live):
    anywhere = pl.BlockSpec(memory_space=pl.ANY)
    anywhere_at_all = pl.BlockSpec(memory_space=pl.ANY)
    rows = B * BLOCKS
    pairs = 3 * BLOCKS
    flops = 10 * pairs * B * B * HD
    grads = pl.pallas_call(
        functools.partial(kernel, lax.axis_size("ctx")),
        out_shape=pltpu.VMEM((3, *queries.shape), jnp.bfloat16),
        in_specs=[
            pl.BlockSpec(memory_space=pltpu.SMEM),
            anywhere,
            anywhere,
            anywhere,
            anywhere,
            anywhere,
            anywhere,
        ],
        out_specs=anywhere,
        scratch_shapes=[
            pltpu.VMEM((4, rows, HD), jnp.bfloat16),
            pltpu.VMEM((BLOCKS * RUNS, 2, HD), jnp.float32),
            pltpu.VMEM((H, 2, HD), jnp.float32),
            pltpu.VMEM((pairs, B, B), jnp.float32),
            pltpu.VMEM((pairs, B, B), jnp.bfloat16),
            pltpu.VMEM((3, rows, HD), jnp.bfloat16),
            pltpu.VMEM((2, RUN, H * HD), jnp.bfloat16),
            pltpu.VMEM((H, RUN), jnp.float32),
            pltpu.SemaphoreType.DMA((3,)),
            pltpu.SemaphoreType.DMA((4,)),
            pltpu.SemaphoreType.DMA((4,)),
            pltpu.SemaphoreType.DMA((2,)),
            pltpu.SemaphoreType.DMA((3,)),
            pltpu.SemaphoreType.DMA((3,)),
        ],
        compiler_params=pltpu.CompilerParams(
            collective_id=0, has_side_effects=True, vmem_limit_bytes=56 * 1024 * 1024
        ),
        cost_estimate=pl.CostEstimate(
            flops=flops, bytes_accessed=8 * RUN * H * HD * 2, transcendentals=pairs * B * B
        ),
        name="pair_attention_backward",
    )(
        pair_live,
        *(
            pltpu.with_memory_space_constraint(array, pltpu.HBM)
            for array in (jnp.transpose(log_totals), queries, keys, values, outputs, grad_out)
        ),
    )
    out = jax.ShapeDtypeStruct(queries.shape, jnp.bfloat16)
    return pl.pallas_call(
        store,
        out_shape=(out, out, out),
        in_specs=[anywhere_at_all],
        out_specs=(anywhere_at_all,) * 3,
        scratch_shapes=[pltpu.SemaphoreType.DMA((3,))],
        name="store_gradients",
    )(grads)


def solution(mesh):
    rows = P(("head", "ctx"), None)
    return jax.shard_map(
        on_device,
        mesh=mesh,
        in_specs=(rows, rows, rows, rows, rows, rows, P()),
        out_specs=(rows, rows, rows),
        check_vma=False,
    )
```

```python
import functools

import jax
import jax.numpy as jnp
from jax import lax
from jax.experimental import pallas as pl
from jax.experimental.pallas import tpu as pltpu
from jax.sharding import PartitionSpec as P

H = 32
HD = 128
RUN = 64
RUNS = 8
BLOCKS = 4
B = RUN * RUNS
LOG2E = 1.4426950408889634
SCALE = 1.0 / HD**0.5
Q, K, DO, V = 0, 1, 2, 3
NT = (((1,), (1,)), ((), ()))
NN = (((1,), (0,)), ((), ()))
TN = (((0,), (0,)), ((), ()))


def dot(a, b, dims):
    return lax.dot_general(a, b, dims, preferred_element_type=jnp.float32)


def partner(block, step):
    if step == 0:
        return block
    if step == 1:
        return block + 1 - 2 * (block % 2)
    return (block + 2) % 4


def kernel(
    ctx_size,
    live_ref,
    lse_ref,
    q_ref,
    k_ref,
    v_ref,
    o_ref,
    do_ref,
    out_ref,
    buf,
    stat,
    stat_src,
    probs,
    grad_s,
    stage,
    rows,
    lse_rows,
    load_sem,
    send_sem,
    recv_sem,
    stat_sem,
    back_send,
    back_recv,
):
    run = lax.axis_index("head")
    ctx = lax.axis_index("ctx")
    quarter = ctx_size // 4
    rest = ctx % quarter
    y_lo = ctx // quarter // 2
    z_hi = ctx // quarter % 2
    y = run // 2 * 2 + y_lo
    core = run % 2
    block = z_hi * 2 + y_lo

    def head(z_there, core_there, y_there):
        return z_there * 16 + core_there * 8 + y_there

    def columns(index):
        return pl.ds(pl.multiple_of(index * HD, HD), HD)

    def device(y_there, core_there, z_there):
        ctx_there = (y_there % 2 * 2 + z_there) * quarter + rest
        return (y_there // 2 * 2 + core_there, ctx_there)

    def send(source, target, sent, received, where):
        pltpu.make_async_remote_copy(
            src_ref=source,
            dst_ref=target,
            send_sem=sent,
            recv_sem=received,
            device_id=where,
            device_id_type=pl.DeviceIdType.MESH,
        ).start()

    def y_at(p):
        i = p // 2
        return (y + 4 + i - i // 2 * (2 * i - 1) + 4 * (p % 2)) % 8

    def each(first, last, body):
        lax.fori_loop(first, last, lambda t, carry: (body(t), carry)[1], 0)

    def place(t):
        return (core + 1 - t % 2) % 2, y_at(t // 4), (z_hi + 1 - t // 2 % 2) % 2

    def peer(t):
        return place(t + (t + 24) // 31)

    barrier = pltpu.get_barrier_semaphore()

    def greet(where):
        pl.semaphore_signal(barrier, inc=1, device_id=where, device_id_type=pl.DeviceIdType.MESH)

    def greet_peer(t):
        core_there, y_there, z_there = peer(t)
        greet(device(y_there, core_there, z_there))

    each(0, 31, greet_peer)
    load_do = pltpu.make_async_copy(do_ref, rows.at[0], load_sem.at[0])
    load_o = pltpu.make_async_copy(o_ref, rows.at[1], load_sem.at[1])
    load_lse = pltpu.make_async_copy(lse_ref, lse_rows, load_sem.at[2])
    load_do.start()
    load_o.start()
    load_lse.start()
    pl.semaphore_wait(barrier, 31)

    def slot(array):
        return buf.at[array, pl.ds(pl.multiple_of((block * RUNS + run) * RUN, RUN), RUN)]

    def send_rows(source, array):
        def body(t):
            core_there, y_there, z_there = peer(t)
            send(
                source.at[:, columns(head(z_there, core_there, y_there))],
                slot(array),
                send_sem.at[array],
                recv_sem.at[array],
                device(y_there, core_there, z_there),
            )

        mine = source.at[:, columns(head(z_hi, core, y))]
        pltpu.make_async_copy(mine, slot(array), recv_sem.at[array]).start()
        each(0, 31, body)

    send_rows(q_ref, Q)
    send_rows(k_ref, K)

    load_do.wait()
    load_o.wait()
    load_lse.wait()
    lanes = lax.broadcasted_iota(jnp.int32, (8, HD), 1)
    half = jnp.where(lanes // RUN == run % 2, 1.0, 0.0).astype(jnp.float32)
    twice = jnp.where(
        lax.broadcasted_iota(jnp.int32, (RUN, HD), 0) == lax.broadcasted_iota(jnp.int32, (RUN, HD), 1) % RUN, 1.0, 0.0
    ).astype(jnp.float32)
    lse_lines = lax.dot_general(
        lse_rows[...], twice, NN, precision=lax.Precision.HIGHEST, preferred_element_type=jnp.float32
    )
    stat_src[:, 0, :] = lse_lines * half[:1]
    ones = jnp.ones((8, 2 * HD), jnp.bfloat16)

    def delta_line(h):
        product = rows[0, :, columns(h)].astype(jnp.float32) * rows[1, :, columns(h)].astype(jnp.float32)
        high = product.astype(jnp.bfloat16)
        low = (product - high.astype(jnp.float32)).astype(jnp.bfloat16)
        both = jnp.concatenate([high, low], axis=1)
        line = dot(ones, jnp.concatenate([both, both], axis=0), NT) * half
        stat_src[h, 1:2, :] = line[:1]

    each(0, H, delta_line)

    def send_stat(t):
        core_there, y_there, z_there = peer(t)
        send(
            stat_src.at[head(z_there, core_there, y_there)],
            stat.at[block * RUNS + run],
            stat_sem.at[0],
            stat_sem.at[1],
            device(y_there, core_there, z_there),
        )

    pltpu.make_async_copy(stat_src.at[head(z_hi, core, y)], stat.at[block * RUNS + run], stat_sem.at[1]).start()
    each(0, 31, send_stat)
    send_rows(do_ref, DO)
    send_rows(v_ref, V)

    def arrived(array):
        pltpu.make_async_copy(buf.at[array], buf.at[array], recv_sem.at[array]).wait()

    def rows_of(array, index):
        return buf[array, pl.ds(pl.multiple_of(index * B, B), B), :]

    def stat_line(index, which):
        parts = []
        for pair in range(RUNS // 2):
            parts.append(
                stat[index * RUNS + 2 * pair, which : which + 1, :]
                + stat[index * RUNS + 2 * pair + 1, which : which + 1, :]
            )
        return jnp.concatenate(parts, axis=1)

    arrived(Q)
    arrived(K)
    pltpu.make_async_copy(stat, stat, stat_sem.at[1]).wait()

    def probs_of(i):
        line = stat_line(i, 0) * LOG2E
        queries = rows_of(Q, i)
        ctx_i = (i % 2 * 2 + i // 2) * quarter + rest
        for step in range(3):
            offset = line
            if step > 0:
                dead = (1 - live_ref[step - 1, ctx_i]).astype(jnp.float32)
                offset = line + dead * 1e30
            keys = rows_of(K, partner(i, step))
            scores = dot(keys, queries, NT) * (SCALE * LOG2E)
            probs[i * 3 + step] = jnp.exp2(scores - offset)

    each(0, BLOCKS, probs_of)

    def staged(array, index):
        return stage.at[array, pl.ds(pl.multiple_of(index * B, B), B)]

    def staged_run(array, index, run_there):
        return stage.at[array, pl.ds(pl.multiple_of((index * RUNS + run_there) * RUN, RUN), RUN)]

    def give_back(array, result_of):
        target = out_ref.at[array, :, columns(head(z_hi, core, y))]

        def half_of_blocks(t):
            odd = 1 - t
            y_there_lo = (y_lo + odd) % 2

            def one_block(z):
                staged(array, z * 2 + y_there_lo)[...] = result_of(z * 2 + y_there_lo).astype(jnp.bfloat16)

            each(0, 2, one_block)

            def body(u):
                v = u + t * ((u + 24) // 31)
                q = v // 4
                core_there, y_there, z_there = place(4 * (q + 2 * odd + t * 4 * (q // 2)) + v % 4)
                send(
                    staged_run(array, z_there * 2 + y_there_lo, y_there // 2 * 2 + core_there),
                    target,
                    back_send.at[array],
                    back_recv.at[array],
                    device(y_there, core_there, z_there),
                )

            each(0, 16 - t, body)

        each(0, 2, half_of_blocks)
        pltpu.make_async_copy(staged_run(array, block, run), target, back_recv.at[array]).start()

    arrived(DO)

    def grad_v_of(j):
        total = jnp.zeros((B, HD), jnp.float32)
        for step in range(3):
            i = partner(j, step)
            total += dot(probs[i * 3 + step].astype(jnp.bfloat16), rows_of(DO, i), NN)
        return total

    give_back(2, grad_v_of)
    arrived(V)

    def grad_k_of(j):
        total = jnp.zeros((B, HD), jnp.float32)
        values = rows_of(V, j)
        for step in range(3):
            i = partner(j, step)
            grad_p = dot(values, rows_of(DO, i), NT)
            grad = (probs[i * 3 + step] * (grad_p - stat_line(i, 1))).astype(jnp.bfloat16)
            grad_s[i * 3 + step] = grad
            total += dot(grad, rows_of(Q, i), NN)
        return total * SCALE

    give_back(1, grad_k_of)

    def grad_q_of(i):
        total = jnp.zeros((B, HD), jnp.float32)
        for step in range(3):
            total += dot(grad_s[i * 3 + step], rows_of(K, partner(i, step)), TN)
        return total * SCALE

    give_back(0, grad_q_of)

    for array in range(4):
        sent = buf.at[array, pl.ds(0, 31 * RUN)]
        pltpu.make_async_copy(sent, sent, send_sem.at[array]).wait()
    pltpu.make_async_copy(stat.at[pl.ds(0, 31)], stat.at[pl.ds(0, 31)], stat_sem.at[0]).wait()
    for array in range(3):
        sent = stage.at[array, pl.ds(0, 31 * RUN)]
        pltpu.make_async_copy(sent, sent, back_send.at[array]).wait()
    for array in range(3):
        pltpu.make_async_copy(out_ref.at[array], out_ref.at[array], back_recv.at[array]).wait()


def store(source, *targets_and_sems):
    *targets, sems = targets_and_sems
    copies = [pltpu.make_async_copy(source.at[i], target, sems.at[i]) for i, target in enumerate(targets)]
    for copy in copies:
        copy.start()
    for copy in copies:
        copy.wait()


def on_device(queries, keys, values, outputs, grad_out, log_totals, pair_live):
    anywhere = pl.BlockSpec(memory_space=pl.ANY)
    anywhere_at_all = pl.BlockSpec(memory_space=pl.ANY)
    rows = B * BLOCKS
    pairs = 3 * BLOCKS
    flops = 10 * pairs * B * B * HD
    grads = pl.pallas_call(
        functools.partial(kernel, lax.axis_size("ctx")),
        out_shape=pltpu.VMEM((3, *queries.shape), jnp.bfloat16),
        in_specs=[
            pl.BlockSpec(memory_space=pltpu.SMEM),
            anywhere,
            anywhere,
            anywhere,
            anywhere,
            anywhere,
            anywhere,
        ],
        out_specs=anywhere,
        scratch_shapes=[
            pltpu.VMEM((4, rows, HD), jnp.bfloat16),
            pltpu.VMEM((BLOCKS * RUNS, 2, HD), jnp.float32),
            pltpu.VMEM((H, 2, HD), jnp.float32),
            pltpu.VMEM((pairs, B, B), jnp.float32),
            pltpu.VMEM((pairs, B, B), jnp.bfloat16),
            pltpu.VMEM((3, rows, HD), jnp.bfloat16),
            pltpu.VMEM((2, RUN, H * HD), jnp.bfloat16),
            pltpu.VMEM((H, RUN), jnp.float32),
            pltpu.SemaphoreType.DMA((3,)),
            pltpu.SemaphoreType.DMA((4,)),
            pltpu.SemaphoreType.DMA((4,)),
            pltpu.SemaphoreType.DMA((2,)),
            pltpu.SemaphoreType.DMA((3,)),
            pltpu.SemaphoreType.DMA((3,)),
        ],
        compiler_params=pltpu.CompilerParams(
            collective_id=0, has_side_effects=True, vmem_limit_bytes=56 * 1024 * 1024
        ),
        cost_estimate=pl.CostEstimate(
            flops=flops, bytes_accessed=8 * RUN * H * HD * 2, transcendentals=pairs * B * B
        ),
        name="pair_attention_backward",
    )(
        pair_live,
        *(
            pltpu.with_memory_space_constraint(array, pltpu.HBM)
            for array in (jnp.transpose(log_totals), queries, keys, values, outputs, grad_out)
        ),
    )
    out = jax.ShapeDtypeStruct(queries.shape, jnp.bfloat16)
    return pl.pallas_call(
        store,
        out_shape=(out, out, out),
        in_specs=[anywhere_at_all],
        out_specs=(anywhere_at_all,) * 3,
        scratch_shapes=[pltpu.SemaphoreType.DMA((3,))],
        name="store_gradients",
    )(pltpu.with_memory_space_constraint(grads, pltpu.VMEM))


def solution(mesh):
    rows = P(("head", "ctx"), None)
    return jax.shard_map(
        on_device,
        mesh=mesh,
        in_specs=(rows, rows, rows, rows, rows, rows, P()),
        out_specs=(rows, rows, rows),
        check_vma=False,
    )
```
